256 devices in a mesh: track: 8 (over z_hi, y), tm: 32 (over z_lo, x, core).
Axes of the slice: x: 4, y: 4, z: 8 (z_hi: 2, z_lo: 4; z = z_hi * 4 + z_lo), core: 2. Of those that a mesh axis runs over, the one named last changes fastest.
Arguments:
- track_query: bfloat16 [16, 4096, 1024], P('track', 'tm'), may hold values from -6 to 6
- track_key: bfloat16 [16, 4096, 1024], P('track', 'tm'), may hold values from -6 to 6
- track_value: bfloat16 [16, 4096, 1024], P('track', 'tm'), may hold values from -6 to 6
- log_decay: float32 [16, 8, 4096], P('track', None, 'tm'), may hold values from -2.3 to 0
- valid_length: int32 [16], replicated, may hold values from 1024 to 4096, as said below
- initial_state: bfloat16 [16, 8, 128, 128], P('track'), may hold values from -24 to 24
- cross_query: bfloat16 [16, 4096, 1024], P('track', 'tm'), may hold values from -5 to 5
- cross_key: bfloat16 [16, 4096, 1024], P('track', 'tm'), may hold values from -5 to 5
- grad_out: bfloat16 [16, 4096, 1024], P('track', 'tm'), may hold values from -6 to 6
Outputs:
- grad_query: bfloat16 [16, 4096, 1024], P('track', 'tm')
- grad_key: bfloat16 [16, 4096, 1024], P('track', 'tm')
- grad_value: bfloat16 [16, 4096, 1024], P('track', 'tm')
- grad_cross_query: bfloat16 [16, 4096, 1024], P('track', 'tm')
- grad_cross_key: bfloat16 [16, 4096, 1024], P('track', 'tm')
The draws below stay inside these ranges and needn't reach their ends.
Inputs may be any that keep to these rules, and one draw needn't show every extreme that they name: `valid_length`: multiples of 128; one track has 4096 valid steps and one has exactly 1024.
All inputs are finite; a program needn't handle non-finite values.
Results may differ from the reference program's by a relative error of at most 0.005.
Values may be sent and summed in bfloat16 or wider, within the bound.
No kernel may reach another device: no remote copies, remote signals or barrier semaphores. Data moves between devices by JAX's collectives and lax.ppermute only.
A program may use at most 192 MiB of HBM per device.

```python
import jax
import jax.numpy as jnp
from jax import lax

H = 8
DH = 128
D = 1024
VOICE_PARTS = 16
SEQUENCE_LENGTH = 4096
SHORT = 1024


def draw_valid_length(key, part):
    first_key, second_key = jax.random.split(jax.random.fold_in(key, 11))
    blocks = jax.random.randint(first_key, (VOICE_PARTS,), SHORT // 128, SEQUENCE_LENGTH // 128 + 1)
    lengths = blocks * 128
    picked = jax.random.permutation(second_key, VOICE_PARTS)
    lengths = lengths.at[picked[0]].set(SEQUENCE_LENGTH)
    lengths = lengths.at[picked[1]].set(SHORT)
    return lengths.astype(jnp.int32)


def draw_log_decay(key, part):
    gathered_lookup_vectors = jax.random.split(jax.random.fold_in(key, 23), 6)
    share_fast = 0.35
    chooser = jax.random.uniform(gathered_lookup_vectors[0], (VOICE_PARTS, H))
    fast_rate = jnp.exp(jax.random.uniform(gathered_lookup_vectors[1], (VOICE_PARTS, H), minval=jnp.log(1.0 / 50.0), maxval=jnp.log(1.0 / 30.0)))
    slow_rate = jnp.exp(jax.random.uniform(gathered_lookup_vectors[2], (VOICE_PARTS, H), minval=jnp.log(0.05 / SEQUENCE_LENGTH), maxval=jnp.log(0.5 / SEQUENCE_LENGTH)))
    head_rate = jnp.where(chooser < share_fast, fast_rate, slow_rate)
    roughness = jnp.exp(jax.random.uniform(gathered_lookup_vectors[3], (VOICE_PARTS, H, SEQUENCE_LENGTH), minval=jnp.log(0.5), maxval=jnp.log(2.0)))
    forget_gate_logarithm = -head_rate[:, :, None] * roughness
    moment_indices = jax.random.randint(gathered_lookup_vectors[4], (VOICE_PARTS, 3), 0, SEQUENCE_LENGTH)
    segment_length = jax.random.uniform(gathered_lookup_vectors[5], (VOICE_PARTS, 3), minval=0.22, maxval=0.69)
    segment_count = jnp.zeros((VOICE_PARTS, SEQUENCE_LENGTH), jnp.float32)
    segment_count = segment_count.at[jnp.arange(VOICE_PARTS)[:, None], moment_indices].add(segment_length)
    return (forget_gate_logarithm - segment_count[:, None, :]).astype(jnp.float32)


def cross_pair(key):
    gathered_lookup_vectors = jax.random.split(jax.random.fold_in(key, 37), 2)
    full_shape = (VOICE_PARTS, SEQUENCE_LENGTH, D)
    query_draw = jnp.clip(jax.random.normal(gathered_lookup_vectors[0], full_shape), -5.0, 5.0)
    key_draw = jnp.clip(jax.random.normal(gathered_lookup_vectors[1], full_shape), -5.0, 5.0)
    return (query_draw, key_draw)


def draw_cross_query(key, part):
    return cross_pair(key)[0].astype(jnp.bfloat16)


def draw_cross_key(key, part):
    return cross_pair(key)[1].astype(jnp.bfloat16)


def block_levels(own_key, extent, pieces, low, high):
    gain = 1.0
    for dim, shards_of in pieces:
        heights = jax.random.uniform(jax.random.fold_in(jax.random.fold_in(own_key, 6), dim), (shards_of,), jnp.float32, low / len(pieces), high / len(pieces))
        gain = gain * jnp.repeat(jnp.exp(heights), extent[dim] // shards_of).reshape((-1,) + (1,) * (len(extent) - 1 - dim))
    return gain


def centred(own_key, extent, deviation, reach, cuts=(), kind=jnp.bfloat16):
    entries = deviation * jax.random.normal(own_key, extent, jnp.float32)
    if cuts:
        entries = entries * block_levels(own_key, extent, cuts, -0.22, 0.18)
    return jnp.clip(entries, -reach, reach).astype(kind)


def setup_inputs(seed: int = 0) -> dict:
    streams_of = jax.random.split(jax.random.key(seed), 10)
    track_query = centred(streams_of[0], (VOICE_PARTS, SEQUENCE_LENGTH, D), 1.0, 6.0, ((0, 8), (1, 32)))
    track_key = centred(streams_of[1], (VOICE_PARTS, SEQUENCE_LENGTH, D), 1.0, 6.0, ((0, 8), (1, 32)))
    track_value = centred(streams_of[2], (VOICE_PARTS, SEQUENCE_LENGTH, D), 1.0, 6.0, ((0, 8), (1, 32)))
    log_decay = draw_log_decay(jax.random.fold_in(streams_of[9], 71), 0)
    valid_length = draw_valid_length(jax.random.fold_in(streams_of[9], 71), 0)
    initial_state = centred(streams_of[5], (VOICE_PARTS, H, DH, DH), 4.0, 24.0, ((0, 8),))
    cross_query = draw_cross_query(jax.random.fold_in(streams_of[9], 71), 0)
    cross_key = draw_cross_key(jax.random.fold_in(streams_of[9], 71), 0)
    grad_out = centred(streams_of[8], (VOICE_PARTS, SEQUENCE_LENGTH, D), 1.0, 6.0, ((0, 8), (1, 32)))
    return {"track_query": track_query, "track_key": track_key, "track_value": track_value, "log_decay": log_decay, "valid_length": valid_length, "initial_state": initial_state, "cross_query": cross_query, "cross_key": cross_key, "grad_out": grad_out}


EPSILON = 1e-06
HIGHEST_PRECISION = lax.Precision.HIGHEST
BLOCK_ROWS = 128

def track_forward(query_rows, key_rows, value_rows, decay_rows, valid_rows, start_state):
    head_count = decay_rows.shape[0]
    total_rows = query_rows.shape[0]
    model_width = query_rows.shape[1]
    head_size = model_width // head_count
    blocks = total_rows // BLOCK_ROWS
    split_shape = (blocks, BLOCK_ROWS, head_count, head_size)
    query_float = query_rows.astype(jnp.float32).reshape(split_shape)
    key_float = (key_rows.astype(jnp.float32) * valid_rows[:, None]).reshape(split_shape)
    value_float = value_rows.astype(jnp.float32).reshape(split_shape)
    decay_split = jnp.transpose(decay_rows.reshape(head_count, blocks, BLOCK_ROWS), (1, 0, 2))
    lower_mask = jnp.arange(BLOCK_ROWS)[:, None] >= jnp.arange(BLOCK_ROWS)[None, :]

    def block_step(carry_state, inputs):
        query_block, key_block, value_block, decay_block = inputs
        within = jnp.cumsum(decay_block, axis=-1)
        decay_matrix = jnp.exp(jnp.where(lower_mask, within[:, :, None] - within[:, None, :], -jnp.inf))
        scores = jnp.einsum('thc,shc->hts', query_block, key_block, precision=HIGHEST_PRECISION) * decay_matrix
        from_start = jnp.transpose(jnp.exp(within))[:, :, None]
        to_end = jnp.transpose(jnp.exp(within[:, -1:] - within))[:, :, None]
        outputs = jnp.einsum('hts,shd->thd', scores, value_block, precision=HIGHEST_PRECISION)
        outputs = outputs + from_start * jnp.einsum('thc,hcd->thd', query_block, carry_state, precision=HIGHEST_PRECISION)
        new_state = jnp.exp(within[:, -1])[:, None, None] * carry_state
        new_state = new_state + jnp.einsum('shc,shd->hcd', key_block * to_end, value_block, precision=HIGHEST_PRECISION)
        return (new_state, outputs)
    initial = start_state.astype(jnp.float32)
    _, outputs = lax.scan(block_step, initial, (query_float, key_float, value_float, decay_split))
    outputs = outputs.reshape(total_rows, head_count, head_size)
    mean_square = lax.optimization_barrier(jnp.mean(outputs * outputs, axis=-1, keepdims=True))
    normed = outputs * (1.0 / jnp.sqrt(mean_square + EPSILON)) * valid_rows[:, None, None]
    return normed.astype(jnp.bfloat16).reshape(total_rows, model_width)

def cross_mix(cross_query, cross_key, normed, valid_mask):
    query_float = cross_query.astype(jnp.float32).reshape(VOICE_PARTS, SEQUENCE_LENGTH, H, DH)
    key_float = cross_key.astype(jnp.float32).reshape(VOICE_PARTS, SEQUENCE_LENGTH, H, DH)
    normed_float = normed.astype(jnp.float32).reshape(VOICE_PARTS, SEQUENCE_LENGTH, H, DH)
    logits = jnp.einsum('ithc,jthc->thij', query_float, key_float, precision=HIGHEST_PRECISION) / float(DH) ** 0.5
    logits = jnp.where(jnp.transpose(valid_mask)[:, None, None, :] > 0, logits, -1e+30)
    weights = jax.nn.softmax(logits, axis=-1)
    mixed = jnp.einsum('thij,jthd->ithd', weights, normed_float, precision=HIGHEST_PRECISION)
    return (mixed * valid_mask[:, :, None, None]).reshape(VOICE_PARTS, SEQUENCE_LENGTH, D)

def reference(track_query, track_key, track_value, log_decay, valid_length, initial_state, cross_query, cross_key, grad_out):
    time_index = jnp.arange(SEQUENCE_LENGTH)
    valid_mask = (time_index[None, :] < valid_length[:, None]).astype(jnp.float32)
    normed = lax.map(lambda packed: track_forward(packed[0], packed[1], packed[2], packed[3], packed[4], packed[5]), (track_query, track_key, track_value, log_decay, valid_mask, initial_state))

    def cross_only(query_in, key_in, normed_in):
        return cross_mix(query_in, key_in, normed_in, valid_mask)
    _, pullback = jax.vjp(cross_only, cross_query, cross_key, normed)
    grad_cross_query, grad_cross_key, grad_normed = pullback(grad_out.astype(jnp.float32))

    def track_backward(packed):

        def forward(query_in, key_in, value_in):
            return track_forward(query_in, key_in, value_in, packed[3], packed[4], packed[6])
        _, track_pull = jax.vjp(forward, packed[0], packed[1], packed[2])
        return track_pull(packed[5])
    grad_query, grad_key, grad_value = lax.map(track_backward, (track_query, track_key, track_value, log_decay, valid_mask, grad_normed, initial_state))
    return (grad_query, grad_key, grad_value, grad_cross_query, grad_cross_key)
```

```python
import functools

import jax
import jax.numpy as jnp
from jax import lax
from jax.experimental import pallas as pl
from jax.experimental.pallas import tpu as pltpu
from jax.sharding import PartitionSpec as P

F32, BF16 = jnp.float32, jnp.bfloat16
EPSILON = 1e-06
NEG = -1e30
H, DH = 8, 128
T = 128
NY, NE, NZ = 4, 8, 4
RY = T // NY
PR = DH + 8
VMEM_LIMIT = 48 * 1024 * 1024

NN = ((1,), (0,))
NT = ((1,), (1,))
TN = ((0,), (0,))


def parts(x):
    if x.dtype == BF16:
        return [x]
    hi = x.astype(BF16)
    return [hi, (x - hi.astype(F32)).astype(BF16)]


def dot(a, b, dims):
    pa, pb = parts(a), parts(b)
    if len(pa) == 2 and len(pb) == 2:
        left, right = [pa[0], pa[0], pa[1]], [pb[0], pb[1], pb[0]]
    else:
        n = max(len(pa), len(pb))
        left = pa * (n // len(pa))
        right = pb * (n // len(pb))
    if len(left) > 1:
        left = jnp.concatenate(left, axis=dims[0][0])
        right = jnp.concatenate(right, axis=dims[1][0])
    else:
        left, right = left[0], right[0]
    return lax.dot_general(left, right, (dims, ((), ())), preferred_element_type=F32)


def sums(ld):
    r = lax.broadcasted_iota(jnp.int32, (T, T), 0)
    c = lax.broadcasted_iota(jnp.int32, (T, T), 1)
    upper = (r <= c).astype(F32)
    lower = (r >= c).astype(F32)
    row = lax.dot_general(
        ld, upper, (NN, ((), ())), precision=lax.Precision.HIGHEST, preferred_element_type=F32
    )
    col = lax.dot_general(
        lower, ld, (NT, ((), ())), precision=lax.Precision.HIGHEST, preferred_element_type=F32
    )
    return row, col, r >= c


def vmem_call(body, out_shape, n_smem, n_in, flops=1 << 28, name=None):
    return pl.pallas_call(
        body,
        out_shape=out_shape,
        in_specs=[pl.BlockSpec(memory_space=pltpu.SMEM)] * n_smem
        + [pl.BlockSpec(memory_space=pltpu.VMEM)] * n_in,
        out_specs=jax.tree.map(lambda _: pl.BlockSpec(memory_space=pltpu.VMEM), out_shape),
        compiler_params=pltpu.CompilerParams(vmem_limit_bytes=VMEM_LIMIT),
        name=name,
    )


def shape(*dims, dtype=F32):
    return jax.ShapeDtypeStruct(dims, dtype)


def cols(h):
    return slice(h * DH, (h + 1) * DH)


def block_state_kernel(valid, ld_ref, k_ref, v_ref, out_ref):
    for x in range(2):
        row, col, _ = sums(ld_ref[x])
        for h in range(H):
            p = x * H + h
            total = row[h : h + 1, T - 1 : T]
            scaled = v_ref[x, :, cols(h)].astype(F32) * jnp.exp(col[T - 1 : T, h : h + 1] - col[:, h : h + 1])
            state = dot(k_ref[x, :, cols(h)], scaled, TN)
            out_ref[p // 2, p % 2, 0:DH, :] = state * valid[x].astype(F32)
            out_ref[p // 2, p % 2, DH:PR, :] = jnp.broadcast_to(total, (PR - DH, DH))


def row_total_kernel(back, in_ref, out_ref):
    for p in range(2):
        order = range(NE - 1, -1, -1) if back else range(NE)
        state, total = None, None
        for e in order:
            ld = in_ref[e, p, DH : DH + 1, :]
            if state is None:
                state, total = in_ref[e, p, 0:DH, :], ld
            else:
                state = jnp.exp(ld) * state + in_ref[e, p, 0:DH, :]
                total = total + ld
        out_ref[p, 0:DH, :] = state
        out_ref[p, DH:PR, :] = jnp.broadcast_to(total, (PR - DH, DH))


def row_starts_kernel(back, at, *refs):
    if back:
        row_ref, far3, far2, far1, out_ref = refs
    else:
        init_ref, row_ref, far3, far2, far1, out_ref = refs
    for p in range(2):
        if back:
            state = jnp.zeros((DH, DH), F32)
        else:
            pair = at[0] * 2 + p
            state = init_ref[pair // H, pair % H].astype(F32)
        for far in (far3, far2, far1):
            state = jnp.exp(far[p, DH : DH + 1, :]) * state + far[p, 0:DH, :]
        for e in range(NE - 1, -1, -1) if back else range(NE):
            out_ref[e, p] = state
            state = jnp.exp(row_ref[e, p, DH : DH + 1, :]) * state + row_ref[e, p, 0:DH, :]


def outputs_kernel(valid, ld_ref, q_ref, k_ref, v_ref, s_ref, out_ref, normed_ref):
    for x in range(2):
        row, col, keep = sums(ld_ref[x])
        flag = valid[x].astype(F32)
        for h in range(H):
            p = x * H + h
            q, k, v = q_ref[x, :, cols(h)], k_ref[x, :, cols(h)], v_ref[x, :, cols(h)]
            decay = jnp.exp(jnp.where(keep, col[:, h : h + 1] - row[h : h + 1, :], -jnp.inf))
            scores = dot(q, k, NT) * (decay * flag)
            out = dot(scores, v, NN) + jnp.exp(col[:, h : h + 1]) * dot(q, s_ref[p // 2, p % 2], NN)
            inverse = 1.0 / jnp.sqrt(jnp.mean(out * out, axis=-1, keepdims=True) + EPSILON)
            out_ref[x, :, cols(h)] = out
            normed = (out * (inverse * flag)).astype(BF16)
            for y in range(NY):
                normed_ref[y, x, :, cols(h)] = normed[y * RY : (y + 1) * RY, :]


def same_time():
    t = lax.broadcasted_iota(jnp.int32, (16, 256), 0)
    lane = lax.broadcasted_iota(jnp.int32, (16, 256), 1)
    return (lane & 15) == t


def take(ref, g, h):
    part = ref[:, :, g * 16 : (g + 1) * 16, cols(h)]
    return part.reshape(128, DH)


def both(own_ref, other_ref, g, h):
    return jnp.concatenate([take(own_ref, g, h), take(other_ref, g, h)], axis=0)


def scaled_logits(key_valid, keys, queries):
    logits = (dot(keys, queries, NT) * (1.0 / float(DH) ** 0.5)).reshape(8, 16, 256)
    return [jnp.where(key_valid[j] > 0, logits[j], NEG) for j in range(8)]


def put(ref, g, h, value):
    value = value.astype(ref.dtype).reshape(NY, 2, 16, DH)
    ref[:, :, g * 16 : (g + 1) * 16, cols(h)] = value


def stats_kernel(key_valid, k_ref, q_ref, qx_ref, max_ref, sum_ref):
    mask = same_time()
    for h in range(H):
        for g in range(RY // 16):
            logits = scaled_logits(key_valid, take(k_ref, g, h), both(q_ref, qx_ref, g, h))
            top = functools.reduce(jnp.maximum, logits)
            total = functools.reduce(jnp.add, [jnp.exp(one - top) for one in logits])
            r = h * (RY // 16) + g
            max_ref[r : r + 1, :] = jnp.sum(jnp.where(mask, top, 0.0), axis=0, keepdims=True)
            sum_ref[r : r + 1, :] = jnp.sum(jnp.where(mask, total, 0.0), axis=0, keepdims=True)


def swap_halves(x):
    return jnp.concatenate([x[:, 128:], x[:, :128]], axis=1)


def weights_of(key_valid, k, q, r, max_ref, sum_ref, maxx_ref, sumx_ref, mask):
    logits = scaled_logits(key_valid, k, q)
    m, mx = max_ref[r : r + 1, :], swap_halves(maxx_ref[r : r + 1, :])
    top = jnp.maximum(m, mx)
    total = sum_ref[r : r + 1, :] * jnp.exp(m - top) + swap_halves(sumx_ref[r : r + 1, :]) * jnp.exp(mx - top)
    inverse = 1.0 / total
    return [jnp.where(mask, jnp.exp(one - top) * inverse, 0.0) for one in logits]


def mix_kernel(key_valid, k_ref, q_ref, qx_ref, n_ref, g_ref, gx_ref, max_ref, sum_ref, maxx_ref, sumx_ref, vi_ref, gn_ref, rd_ref):
    mask = same_time()
    vi = vi_ref[0:1, :]
    for h in range(H):
        for g in range(RY // 16):
            r = h * (RY // 16) + g
            weights = weights_of(
                key_valid, take(k_ref, g, h), both(q_ref, qx_ref, g, h), r, max_ref, sum_ref, maxx_ref, sumx_ref, mask
            )
            grads = both(g_ref, gx_ref, g, h)
            grad_weights = dot(take(n_ref, g, h), grads, NT).reshape(8, 16, 256)
            weights = [one * vi for one in weights]
            put(gn_ref, g, h, dot(jnp.concatenate(weights, axis=0), grads, NN))
            total = functools.reduce(jnp.add, [weights[j] * grad_weights[j] for j in range(8)])
            rd_ref[r : r + 1, :] = jnp.sum(total, axis=0, keepdims=True)


def cross_grads_kernel(
    key_valid, k_ref, q_ref, qx_ref, n_ref, g_ref, gx_ref, max_ref, sum_ref, maxx_ref, sumx_ref, vi_ref, rd_ref, rdx_ref,
    gk_ref, gq_ref, gqx_ref,
):
    mask = same_time()
    vi = vi_ref[0:1, :]
    for h in range(H):
        for g in range(RY // 16):
            r = h * (RY // 16) + g
            keys, queries = take(k_ref, g, h), both(q_ref, qx_ref, g, h)
            weights = weights_of(key_valid, keys, queries, r, max_ref, sum_ref, maxx_ref, sumx_ref, mask)
            grads = both(g_ref, gx_ref, g, h)
            grad_weights = dot(take(n_ref, g, h), grads, NT).reshape(8, 16, 256)
            along = rd_ref[r : r + 1, :] + swap_halves(rdx_ref[r : r + 1, :])
            scale = vi * (1.0 / float(DH) ** 0.5)
            grad_logits = jnp.concatenate(
                [weights[j] * (grad_weights[j] - along) * scale for j in range(8)], axis=0
            )
            put(gk_ref, g, h, dot(grad_logits, queries, NN))
            grad_queries = dot(grad_logits, keys, TN)
            put(gq_ref, g, h, grad_queries[:128])
            put(gqx_ref, g, h, grad_queries[128:])


def join_kernel(gq_ref, gqx_ref, gk_ref, out_ref):
    for y in range(NY):
        out_ref[y, 0] = (gq_ref[y] + gqx_ref[y].astype(F32)).astype(BF16)
        out_ref[y, 1] = gk_ref[y]


def grad_outputs_kernel(valid, ld_ref, q_ref, out_ref, gn_ref, go_ref, msg_ref):
    for x in range(2):
        row, col, _ = sums(ld_ref[x])
        flag = valid[x].astype(F32)
        for h in range(H):
            p = x * H + h
            out = out_ref[x, :, cols(h)]
            grad = jnp.concatenate([gn_ref[y, x, :, cols(h)] for y in range(NY)], axis=0).astype(F32)
            inverse = 1.0 / jnp.sqrt(jnp.mean(out * out, axis=-1, keepdims=True) + EPSILON)
            along = jnp.sum(grad * out, axis=-1, keepdims=True)
            go = flag * (inverse * grad - (inverse * inverse * inverse * (1.0 / DH) * along) * out)
            go_ref[x, :, cols(h)] = go
            scaled = go * jnp.exp(col[:, h : h + 1])
            msg_ref[p // 2, p % 2, 0:DH, :] = dot(q_ref[x, :, cols(h)], scaled, TN)
            msg_ref[p // 2, p % 2, DH:PR, :] = jnp.broadcast_to(row[h : h + 1, T - 1 : T], (PR - DH, DH))


def local_grads_kernel(valid, ld_ref, q_ref, k_ref, v_ref, s_ref, go_ref, gq_ref, gk_ref, gv_ref):
    for x in range(2):
        row, col, keep = sums(ld_ref[x])
        flag = valid[x].astype(F32)
        for h in range(H):
            p = x * H + h
            q, k, v = q_ref[x, :, cols(h)], k_ref[x, :, cols(h)], v_ref[x, :, cols(h)]
            go = go_ref[x, :, cols(h)]
            decay = jnp.exp(jnp.where(keep, col[:, h : h + 1] - row[h : h + 1, :], -jnp.inf)) * flag
            scores = dot(q, k, NT) * decay
            grad_scores = dot(go, v, NT) * decay
            gq = dot(grad_scores, k, NN) + jnp.exp(col[:, h : h + 1]) * dot(go, s_ref[p // 2, p % 2], NT)
            gq_ref[x, :, cols(h)] = gq.astype(BF16)
            gk_ref[x, :, cols(h)] = dot(grad_scores, q, TN)
            gv_ref[x, :, cols(h)] = dot(scores, go, TN)


def final_kernel(valid, ld_ref, k_ref, v_ref, gk_in, gv_in, s_ref, gk_ref, gv_ref):
    for x in range(2):
        row, col, _ = sums(ld_ref[x])
        flag = valid[x].astype(F32)
        for h in range(H):
            p = x * H + h
            k, v = k_ref[x, :, cols(h)], v_ref[x, :, cols(h)]
            to_end = jnp.exp(col[T - 1 : T, h : h + 1] - col[:, h : h + 1]) * flag
            state = s_ref[p // 2, p % 2]
            gk_ref[x, :, cols(h)] = (gk_in[x, :, cols(h)] * flag + to_end * dot(v, state, NT)).astype(BF16)
            gv_ref[x, :, cols(h)] = (gv_in[x, :, cols(h)] * flag + to_end * dot(k, state, NN)).astype(BF16)


ROWS = [[z * NE + e for e in range(NE)] for z in range(NZ)]
YS = [[half * NY + y for y in range(NY)] for half in range(2)]
SWAP = [(i, (i + NY) % (2 * NY)) for i in range(2 * NY)]


def to_rows(x):
    return lax.all_to_all(x, "tm", 0, 0, axis_index_groups=ROWS, tiled=True)


def over_y(x):
    return lax.all_to_all(x, "track", 0, 0, axis_index_groups=YS, tiled=True)


def swap(x):
    return lax.ppermute(x, "track", SWAP)


def z_shift(x, step):
    pairs = [
        (z * NE + e, (z + step) * NE + e) for z in range(NZ) for e in range(NE) if 0 <= z + step < NZ
    ]
    return lax.ppermute(x, "tm", pairs)


def scan_states(message, at, initial, back):
    row = to_rows(message)
    total = vmem_call(functools.partial(row_total_kernel, back), shape(2, PR, DH), 0, 1)(row)
    sign = -1 if back else 1
    far = [z_shift(total, sign * step) for step in (3, 2, 1)]
    starts = vmem_call(
        functools.partial(row_starts_kernel, back), shape(NE, 2, DH, DH), 1, 4 if back else 5
    )(at, *(() if back else (initial,)), row, *far)
    return to_rows(starts)


def per_device(q, k, v, log_decay, valid_length, initial, cross_q, cross_k, grad_out):
    tm, track = lax.axis_index("tm"), lax.axis_index("track")
    half, first = track // NY, tm * T
    alive = (first < valid_length).astype(jnp.int32)
    own_valid = lax.dynamic_slice(alive, (2 * track,), (2,))
    half_valid = lax.dynamic_slice(alive, (8 * half,), (8,))
    other_valid = lax.dynamic_slice(alive, (8 * (1 - half),), (8,))
    lanes = jnp.repeat(jnp.concatenate([half_valid, other_valid]).astype(F32), 16)
    vi = jnp.broadcast_to(lanes[None, :], (8, 256))
    at = jnp.stack([tm % NE, tm // NE]).astype(jnp.int32)

    def rows_of(x):
        return x.reshape(2, NY, RY, H * DH).transpose(1, 0, 2, 3)

    message = vmem_call(block_state_kernel, shape(NE, 2, PR, DH), 1, 3)(own_valid, log_decay, k, v)
    cq, go_in = over_y(rows_of(cross_q)), over_y(rows_of(grad_out))
    ck = over_y(rows_of(cross_k))
    cqx, gox = swap(cq), swap(go_in)

    state = scan_states(message, at, initial, False)
    out, normed = vmem_call(
        outputs_kernel, (shape(2, T, H * DH), shape(NY, 2, RY, H * DH, dtype=BF16)), 1, 5
    )(own_valid, log_decay, q, k, v, state)
    n_rows = RY // 16 * H
    tops, totals = vmem_call(stats_kernel, (shape(n_rows, 256), shape(n_rows, 256)), 1, 3)(half_valid, ck, cq, cqx)
    topsx, totalsx = swap(tops), swap(totals)
    nx = over_y(normed)
    quarter = shape(NY, 2, RY, H * DH, dtype=BF16)
    cross_in = (half_valid, ck, cq, cqx, nx, go_in, gox, tops, totals, topsx, totalsx, vi)
    gn, rd = vmem_call(mix_kernel, (quarter, shape(n_rows, 256)), 1, 11)(*cross_in)
    gn_t = over_y(gn)
    rdx = swap(rd)
    gk_x, gq_own, gq_other = vmem_call(
        cross_grads_kernel, (quarter, shape(NY, 2, RY, H * DH), quarter), 1, 13
    )(*cross_in, rd, rdx)
    gq_back = swap(gq_other)

    go, back_message = vmem_call(grad_outputs_kernel, (shape(2, T, H * DH), shape(NE, 2, PR, DH)), 1, 4)(
        own_valid, log_decay, q, out, gn_t
    )
    state_grad = scan_states(back_message, at, None, True)
    whole = shape(2, T, H * DH)
    half_whole = shape(2, T, H * DH, dtype=BF16)
    grad_q, gk_local, gv_local = vmem_call(local_grads_kernel, (half_whole, whole, whole), 1, 6)(
        own_valid, log_decay, q, k, v, state, go
    )
    grad_k, grad_v = vmem_call(final_kernel, (half_whole, half_whole), 1, 6)(
        own_valid, log_decay, k, v, gk_local, gv_local, state_grad
    )
    joined = vmem_call(join_kernel, shape(NY, 2, 2, RY, H * DH, dtype=BF16), 0, 3)(gq_own, gq_back, gk_x)
    joined = over_y(joined)
    grad_cross = joined.transpose(1, 2, 0, 3, 4).reshape(2, 2, T, H * DH)
    return grad_q, grad_k, grad_v, grad_cross[0], grad_cross[1]


def solution(mesh):
    rows = P("track", "tm", None)
    return jax.shard_map(
        per_device,
        mesh=mesh,
        in_specs=(rows, rows, rows, P("track", None, "tm"), P(), P("track", None, None, None), rows, rows, rows),
        out_specs=(rows,) * 5,
        check_vma=False,
    )
```

```python
import functools

import jax
import jax.numpy as jnp
from jax import lax
from jax.experimental import pallas as pl
from jax.experimental.pallas import tpu as pltpu
from jax.sharding import PartitionSpec as P

F32, BF16 = jnp.float32, jnp.bfloat16
EPSILON = 1e-06
NEG = -1e30
H, DH = 8, 128
T = 128
NY, NX, NZ = 4, 4, 4
RY = T // NY
PR = DH + 8
PZ = DH + 16
VMEM_LIMIT = 48 * 1024 * 1024

NN = ((1,), (0,))
NT = ((1,), (1,))
TN = ((0,), (0,))


def parts(x):
    if x.dtype == BF16:
        return [x]
    hi = x.astype(BF16)
    return [hi, (x - hi.astype(F32)).astype(BF16)]


def dot(a, b, dims):
    pa, pb = parts(a), parts(b)
    if len(pa) == 2 and len(pb) == 2:
        left, right = [pa[0], pa[0], pa[1]], [pb[0], pb[1], pb[0]]
    else:
        n = max(len(pa), len(pb))
        left = pa * (n // len(pa))
        right = pb * (n // len(pb))
    if len(left) > 1:
        left = jnp.concatenate(left, axis=dims[0][0])
        right = jnp.concatenate(right, axis=dims[1][0])
    else:
        left, right = left[0], right[0]
    return lax.dot_general(left, right, (dims, ((), ())), preferred_element_type=F32)


def sums(ld):
    r = lax.broadcasted_iota(jnp.int32, (T, T), 0)
    c = lax.broadcasted_iota(jnp.int32, (T, T), 1)
    upper = (r <= c).astype(F32)
    lower = (r >= c).astype(F32)
    row = lax.dot_general(
        ld, upper, (NN, ((), ())), precision=lax.Precision.HIGHEST, preferred_element_type=F32
    )
    col = lax.dot_general(
        lower, ld, (NT, ((), ())), precision=lax.Precision.HIGHEST, preferred_element_type=F32
    )
    return row, col, r >= c


def vmem_call(body, out_shape, n_smem, n_in, scratch=(), after=()):
    n = n_smem + n_in

    def ordered(*refs):
        body(*refs[:n], *refs[n + len(after) :])

    call = pl.pallas_call(
        ordered,
        out_shape=out_shape,
        in_specs=[pl.BlockSpec(memory_space=pltpu.SMEM)] * n_smem
        + [pl.BlockSpec(memory_space=pltpu.VMEM)] * n_in
        + [pl.BlockSpec(memory_space=pl.ANY)] * len(after),
        out_specs=jax.tree.map(lambda _: pl.BlockSpec(memory_space=pltpu.VMEM), out_shape),
        scratch_shapes=scratch,
        compiler_params=pltpu.CompilerParams(vmem_limit_bytes=VMEM_LIMIT),
    )
    return lambda *args: call(*args, *after)


def shape(*dims, dtype=F32):
    return jax.ShapeDtypeStruct(dims, dtype)


def cols(h):
    return slice(h * DH, (h + 1) * DH)


def store_message(ref, h, state, total):
    ref[h, 0:DH, :] = state
    ref[h, DH:PR, :] = jnp.broadcast_to(total, (PR - DH, DH))


def pack_kernel(*refs):
    *ins, out_ref = refs
    for i, one in enumerate(ins):
        for y in range(NY):
            out_ref[y, i] = one[:, y * RY : (y + 1) * RY, :]


def pack(*arrays, after=()):
    n = len(arrays)
    return vmem_call(pack_kernel, shape(NY, n, 2, RY, H * DH, dtype=BF16), 0, n, after=after)(*arrays)


def block_state_kernel(at, valid, ld_ref, k_ref, v_ref, keep_ref, send_ref):
    for i, out_ref in enumerate((keep_ref, send_ref)):
        x = at[0] if i == 0 else 1 - at[0]
        row, col, _ = sums(ld_ref[x])
        for h in range(H):
            scaled = v_ref[x, :, cols(h)].astype(F32) * jnp.exp(col[T - 1 : T, h : h + 1] - col[:, h : h + 1])
            state = dot(k_ref[x, :, cols(h)], scaled, TN)
            store_message(out_ref, h, state * valid[x].astype(F32), row[h : h + 1, T - 1 : T])


def chip_total_kernel(back, at, mine_ref, theirs_ref, *out_refs):
    first = at[0] == (1 if back else 0)
    for q, out_ref in enumerate(out_refs):
        for i in range(2):
            h = 2 * lax.rem(at[1] + q, NX) + i
            mine, theirs = mine_ref[h, DH : DH + 1, :], theirs_ref[h, DH : DH + 1, :]
            a = jnp.where(first, jnp.exp(theirs), 1.0)
            b = jnp.where(first, 1.0, jnp.exp(mine))
            store_message(out_ref, i, a * mine_ref[h, 0:DH, :] + b * theirs_ref[h, 0:DH, :], mine + theirs)


def row_total_kernel(back, at, *refs):
    *in_refs, row_ref, out_ref = refs
    for q, one in enumerate(in_refs):
        row_ref[lax.rem(at[1] - q + NX, NX)] = one[...]
    for p in range(2):
        state, total = None, None
        for j in range(NX - 1, -1, -1) if back else range(NX):
            ld = row_ref[j, p, DH : DH + 1, :]
            if state is None:
                state, total = row_ref[j, p, 0:DH, :], ld
            else:
                state = jnp.exp(ld) * state + row_ref[j, p, 0:DH, :]
                total = total + ld
        high = total.astype(BF16).astype(F32)
        middle = (total - high).astype(BF16).astype(F32)
        r = lax.broadcasted_iota(jnp.int32, (PZ - DH, DH), 0)
        pieces = jnp.where(r == 0, high, jnp.where(r == 1, middle, jnp.where(r == 2, total - high - middle, 0.0)))
        out_ref[p] = jnp.concatenate([state, pieces], axis=0).astype(BF16)


def row_starts_kernel(back, at, *refs):
    if back:
        row_ref, far3, far2, far1, *out_refs, starts = refs
    else:
        init_ref, row_ref, far3, far2, far1, *out_refs, starts = refs
    for p in range(2):
        if back:
            state = jnp.zeros((DH, DH), F32)
        else:
            state = init_ref[at[0], 2 * at[1] + p].astype(F32)
        for far in (far3, far2, far1):
            one = far[p].astype(F32)
            state = jnp.exp(jnp.sum(one[DH:PZ], axis=0, keepdims=True)) * state + one[0:DH]
        for j in range(NX - 1, -1, -1) if back else range(NX):
            starts[j, p] = state
            state = jnp.exp(row_ref[j, p, DH : DH + 1, :]) * state + row_ref[j, p, 0:DH, :]
    for q, out_ref in enumerate(out_refs):
        out_ref[...] = starts[lax.rem(at[1] + q, NX)]


def core_starts_kernel(back, at, *refs):
    *in_refs, mine_ref, theirs_ref, keep_ref, send_ref = refs
    first = at[0] == (1 if back else 0)
    on, off = jnp.where(first, 1.0, 0.0), jnp.where(first, 0.0, 1.0)
    for q, one in enumerate(in_refs):
        for i in range(2):
            h = 2 * lax.rem(at[1] - q + NX, NX) + i
            state = one[i]
            mine, theirs = mine_ref[h, DH : DH + 1, :], theirs_ref[h, DH : DH + 1, :]
            keep_ref[h] = jnp.where(first, 1.0, jnp.exp(theirs)) * state + off * theirs_ref[h, 0:DH, :]
            send_ref[h] = jnp.where(first, jnp.exp(mine), 1.0) * state + on * mine_ref[h, 0:DH, :]


def outputs_kernel(at, valid, ld_ref, q_ref, k_ref, v_ref, *refs):
    *s_refs, out_ref, normed_ref = refs
    for i, s_ref in enumerate(s_refs):
        x = at[0] if i == 0 else 1 - at[0]
        row, col, keep = sums(ld_ref[x])
        flag = valid[x].astype(F32)
        for h in range(H):
            q, k, v = q_ref[x, :, cols(h)], k_ref[x, :, cols(h)], v_ref[x, :, cols(h)]
            decay = jnp.exp(jnp.where(keep, col[:, h : h + 1] - row[h : h + 1, :], -jnp.inf))
            scores = dot(q, k, NT) * (decay * flag)
            out = dot(scores, v, NN) + jnp.exp(col[:, h : h + 1]) * dot(q, s_ref[h], NN)
            inverse = 1.0 / jnp.sqrt(jnp.mean(out * out, axis=-1, keepdims=True) + EPSILON)
            out_ref[x, :, cols(h)] = out
            normed = (out * (inverse * flag)).astype(BF16)
            for y in range(NY):
                normed_ref[y, 0, x, :, cols(h)] = normed[y * RY : (y + 1) * RY, :]


def same_time():
    t = lax.broadcasted_iota(jnp.int32, (16, 256), 0)
    lane = lax.broadcasted_iota(jnp.int32, (16, 256), 1)
    return (lane & 15) == t


def take(ref, g, h, i=0):
    part = ref[:, i, :, g * 16 : (g + 1) * 16, cols(h)]
    return part.reshape(128, DH)


def queries_of(qqk_ref, g, h):
    return jnp.concatenate([take(qqk_ref, g, h, 0), take(qqk_ref, g, h, 1)], axis=0)


def grads_of(g_ref, gx_ref, g, h):
    return jnp.concatenate([take(g_ref, g, h), take(gx_ref, g, h)], axis=0)


def scaled_logits(key_valid, keys, queries):
    logits = (dot(keys, queries, NT) * (1.0 / float(DH) ** 0.5)).reshape(8, 16, 256)
    return [jnp.where(key_valid[j] > 0, logits[j], NEG) for j in range(8)]


def put(ref, g, h, value):
    value = value.astype(ref.dtype).reshape(NY, 2, 16, DH)
    ref[:, 0, :, g * 16 : (g + 1) * 16, cols(h)] = value


def stats_kernel(key_valid, qqk_ref, max_ref, sum_ref):
    mask = same_time()
    for h in range(H):
        for g in range(RY // 16):
            logits = scaled_logits(key_valid, take(qqk_ref, g, h, 2), queries_of(qqk_ref, g, h))
            top = functools.reduce(jnp.maximum, logits)
            total = functools.reduce(jnp.add, [jnp.exp(one - top) for one in logits])
            r = h * (RY // 16) + g
            max_ref[r : r + 1, :] = jnp.sum(jnp.where(mask, top, 0.0), axis=0, keepdims=True)
            sum_ref[r : r + 1, :] = jnp.sum(jnp.where(mask, total, 0.0), axis=0, keepdims=True)


def swap_halves(x):
    return jnp.concatenate([x[:, 128:], x[:, :128]], axis=1)


def weights_of(key_valid, k, q, r, max_ref, sum_ref, maxx_ref, sumx_ref, mask):
    logits = scaled_logits(key_valid, k, q)
    m, mx = max_ref[r : r + 1, :], swap_halves(maxx_ref[r : r + 1, :])
    top = jnp.maximum(m, mx)
    total = sum_ref[r : r + 1, :] * jnp.exp(m - top) + swap_halves(sumx_ref[r : r + 1, :]) * jnp.exp(mx - top)
    inverse = 1.0 / total
    return [jnp.where(mask, jnp.exp(one - top) * inverse, 0.0) for one in logits]


def mix_kernel(key_valid, qqk_ref, g_ref, gx_ref, n_ref, max_ref, sum_ref, maxx_ref, sumx_ref, vi_ref, gn_ref, rd_ref):
    mask = same_time()
    vi = vi_ref[0:1, :]
    for h in range(H):
        for g in range(RY // 16):
            r = h * (RY // 16) + g
            weights = weights_of(
                key_valid, take(qqk_ref, g, h, 2), queries_of(qqk_ref, g, h), r, max_ref, sum_ref, maxx_ref, sumx_ref, mask
            )
            grads = grads_of(g_ref, gx_ref, g, h)
            grad_weights = dot(take(n_ref, g, h), grads, NT).reshape(8, 16, 256)
            weights = [one * vi for one in weights]
            put(gn_ref, g, h, dot(jnp.concatenate(weights, axis=0), grads, NN))
            total = functools.reduce(jnp.add, [weights[j] * grad_weights[j] for j in range(8)])
            rd_ref[r : r + 1, :] = jnp.sum(total, axis=0, keepdims=True)


def cross_grads_kernel(
    key_valid, qqk_ref, g_ref, gx_ref, n_ref, max_ref, sum_ref, maxx_ref, sumx_ref, vi_ref, rd_ref, rdx_ref,
    gk_ref, gq_ref, gqx_ref,
):
    mask = same_time()
    vi = vi_ref[0:1, :]
    for h in range(H):
        for g in range(RY // 16):
            r = h * (RY // 16) + g
            keys, queries = take(qqk_ref, g, h, 2), queries_of(qqk_ref, g, h)
            weights = weights_of(key_valid, keys, queries, r, max_ref, sum_ref, maxx_ref, sumx_ref, mask)
            grads = grads_of(g_ref, gx_ref, g, h)
            grad_weights = dot(take(n_ref, g, h), grads, NT).reshape(8, 16, 256)
            along = rd_ref[r : r + 1, :] + swap_halves(rdx_ref[r : r + 1, :])
            scale = vi * (1.0 / float(DH) ** 0.5)
            grad_logits = jnp.concatenate(
                [weights[j] * (grad_weights[j] - along) * scale for j in range(8)], axis=0
            )
            put(gk_ref, g, h, dot(grad_logits, queries, NN))
            grad_queries = dot(grad_logits, keys, TN)
            put(gq_ref, g, h, grad_queries[:128])
            put(gqx_ref, g, h, grad_queries[128:])


def join_kernel(gq_ref, gqx_ref, gk_ref, out_ref):
    for y in range(NY):
        out_ref[y, 0] = (gq_ref[y, 0] + gqx_ref[y, 0].astype(F32)).astype(BF16)
        out_ref[y, 1] = gk_ref[y, 0]


def grad_outputs_kernel(at, valid, ld_ref, q_ref, out_ref, gn_ref, go_ref, keep_ref, send_ref):
    for i, msg_ref in enumerate((keep_ref, send_ref)):
        x = at[0] if i == 0 else 1 - at[0]
        row, col, _ = sums(ld_ref[x])
        flag = valid[x].astype(F32)
        for h in range(H):
            out = out_ref[x, :, cols(h)]
            grad = jnp.concatenate([gn_ref[y, 0, x, :, cols(h)] for y in range(NY)], axis=0).astype(F32)
            inverse = 1.0 / jnp.sqrt(jnp.mean(out * out, axis=-1, keepdims=True) + EPSILON)
            along = jnp.sum(grad * out, axis=-1, keepdims=True)
            go = flag * (inverse * grad - (inverse * inverse * inverse * (1.0 / DH) * along) * out)
            go_ref[x, :, cols(h)] = go
            scaled = go * jnp.exp(col[:, h : h + 1])
            store_message(msg_ref, h, dot(q_ref[x, :, cols(h)], scaled, TN), row[h : h + 1, T - 1 : T])


def local_grads_kernel(at, valid, ld_ref, q_ref, k_ref, v_ref, go_ref, *refs):
    *s_refs, gq_ref, gk_ref, gv_ref = refs
    for i, s_ref in enumerate(s_refs):
        x = at[0] if i == 0 else 1 - at[0]
        row, col, keep = sums(ld_ref[x])
        flag = valid[x].astype(F32)
        for h in range(H):
            q, k, v = q_ref[x, :, cols(h)], k_ref[x, :, cols(h)], v_ref[x, :, cols(h)]
            go = go_ref[x, :, cols(h)]
            decay = jnp.exp(jnp.where(keep, col[:, h : h + 1] - row[h : h + 1, :], -jnp.inf)) * flag
            scores = dot(q, k, NT) * decay
            grad_scores = dot(go, v, NT) * decay
            gq = dot(grad_scores, k, NN) + jnp.exp(col[:, h : h + 1]) * dot(go, s_ref[h], NT)
            gq_ref[x, :, cols(h)] = gq.astype(BF16)
            gk_ref[x, :, cols(h)] = dot(grad_scores, q, TN)
            gv_ref[x, :, cols(h)] = dot(scores, go, TN)


def final_kernel(at, valid, ld_ref, k_ref, v_ref, gk_in, gv_in, *refs):
    *s_refs, gk_ref, gv_ref = refs
    for i, s_ref in enumerate(s_refs):
        x = at[0] if i == 0 else 1 - at[0]
        row, col, _ = sums(ld_ref[x])
        flag = valid[x].astype(F32)
        for h in range(H):
            k, v = k_ref[x, :, cols(h)], v_ref[x, :, cols(h)]
            to_end = jnp.exp(col[T - 1 : T, h : h + 1] - col[:, h : h + 1]) * flag
            state = s_ref[h]
            gk_ref[x, :, cols(h)] = (gk_in[x, :, cols(h)] * flag + to_end * dot(v, state, NT)).astype(BF16)
            gv_ref[x, :, cols(h)] = (gv_in[x, :, cols(h)] * flag + to_end * dot(k, state, NN)).astype(BF16)


YS = [[half * NY + y for y in range(NY)] for half in range(2)]
SWAP = [(i, (i + NY) % (2 * NY)) for i in range(2 * NY)]


def over_y(x):
    return lax.all_to_all(x, "track", 0, 0, axis_index_groups=YS, tiled=True)


def swap(x):
    return lax.ppermute(x, "track", SWAP)


def over_tm(x, to):
    pairs = []
    for i in range(NZ * NX * 2):
        place = to(i // (2 * NX), i // 2 % NX, i % 2)
        if place is not None:
            pairs.append((i, (place[0] * NX + place[1]) * 2 + place[2]))
    return lax.ppermute(x, "tm", pairs)


def core_swap(x):
    return over_tm(x, lambda z, x, c: (z, x, 1 - c))


def x_shift(x, step):
    return over_tm(x, lambda z, x, c: (z, (x + step) % NX, c)) if step else x


def z_shift(x, step):
    return over_tm(x, lambda z, x, c: (z + step, x, c) if 0 <= z + step < NZ else None)


def chip_totals(mine, send, at, back):
    theirs = core_swap(send)
    totals = vmem_call(functools.partial(chip_total_kernel, back), (shape(2, PR, DH),) * NX, 1, 2)(at, mine, theirs)
    return theirs, [x_shift(one, q) for q, one in enumerate(totals)]


def earlier_rows(totals, at, back, after):
    row, total = vmem_call(
        functools.partial(row_total_kernel, back),
        (shape(NX, 2, PR, DH), shape(2, PZ, DH, dtype=BF16)),
        1,
        NX,
        after=after,
    )(at, *totals)
    sign = -1 if back else 1
    return row, [z_shift(total, sign * step) for step in (3, 2, 1)]


def chip_starts(row, far, at, initial, back, after):
    own = () if back else (initial,)
    starts = vmem_call(
        functools.partial(row_starts_kernel, back),
        (shape(2, DH, DH),) * NX,
        1,
        len(own) + 4,
        scratch=[pltpu.VMEM((NX, 2, DH, DH), F32)],
        after=after,
    )(at, *own, row, *far)
    return [x_shift(one, q) for q, one in enumerate(starts)]


def core_starts(starts, mine, theirs, at, back, after=()):
    keep, give = vmem_call(
        functools.partial(core_starts_kernel, back), (shape(H, DH, DH),) * 2, 1, NX + 2, after=after
    )(at, *starts, mine, theirs)
    return keep, core_swap(give)


def per_device(q, k, v, log_decay, valid_length, initial, cross_q, cross_k, grad_out):
    tm, track = lax.axis_index("tm"), lax.axis_index("track")
    half, first = track // NY, tm * T
    alive = (first < valid_length).astype(jnp.int32)
    own_valid = lax.dynamic_slice(alive, (2 * track,), (2,))
    half_valid = lax.dynamic_slice(alive, (8 * half,), (8,))
    other_valid = lax.dynamic_slice(alive, (8 * (1 - half),), (8,))
    lanes = jnp.repeat(jnp.concatenate([half_valid, other_valid]).astype(F32), 16)
    vi = jnp.broadcast_to(lanes[None, :], (8, 256))
    at = jnp.stack([tm % 2, tm // 2 % NX, tm // (2 * NX)]).astype(jnp.int32)

    message = (shape(H, PR, DH),) * 2
    whole = shape(2, T, H * DH)
    half_whole = shape(2, T, H * DH, dtype=BF16)
    quarter = shape(NY, 1, 2, RY, H * DH, dtype=BF16)
    row_stats = shape(RY // 16 * H, 256)

    raw_qx = swap(cross_q)
    packed_g = pack(grad_out)
    gy = over_y(packed_g)
    mine, send = vmem_call(block_state_kernel, message, 2, 3, after=(packed_g,))(at, own_valid, log_decay, k, v)
    theirs, totals = chip_totals(mine, send, at, False)
    row, far = earlier_rows(totals, at, False, (raw_qx,))
    packed_q = pack(cross_q, raw_qx, cross_k)
    qqk = over_y(packed_q)
    starts = chip_starts(row, far, at, initial, False, (packed_q,))
    gy, _ = lax.optimization_barrier((gy, far[0]))
    gx = swap(gy)
    states = core_starts(starts, mine, theirs, at, False)
    tops, sums_ = vmem_call(stats_kernel, (row_stats, row_stats), 1, 1)(half_valid, qqk)
    topsx, sumsx = swap(tops), swap(sums_)
    out, normed = vmem_call(outputs_kernel, (whole, quarter), 2, 6, after=(tops,))(
        at, own_valid, log_decay, q, k, v, *states
    )
    nx = over_y(normed)
    cross_in = (half_valid, qqk, gy, gx, nx, tops, sums_, topsx, sumsx, vi)
    gn, rd = vmem_call(mix_kernel, (quarter, row_stats), 1, 9)(*cross_in)
    gn_t = over_y(gn)
    rdx = swap(rd)
    gk_x, gq_own, gq_other = vmem_call(cross_grads_kernel, (quarter, shape(NY, 1, 2, RY, H * DH), quarter), 1, 11)(
        *cross_in, rd, rdx
    )
    gq_back = swap(gq_other)
    go, mine, send = vmem_call(grad_outputs_kernel, (whole, *message), 2, 4, after=(gq_other,))(
        at, own_valid, log_decay, q, out, gn_t
    )
    theirs, totals = chip_totals(mine, send, at, True)
    row, far = earlier_rows(totals, at, True, (gq_back,))
    joined = vmem_call(join_kernel, shape(NY, 2, 2, RY, H * DH, dtype=BF16), 0, 3)(gq_own, gq_back, gk_x)
    starts = chip_starts(row, far, at, None, True, (joined,))
    joined = over_y(joined)
    grad_q, gk_local, gv_local = vmem_call(local_grads_kernel, (half_whole, whole, whole), 2, 7)(
        at, own_valid, log_decay, q, k, v, go, *states
    )
    state_grads = core_starts(starts, mine, theirs, at, True, (grad_q,))
    grad_k, grad_v = vmem_call(final_kernel, (half_whole, half_whole), 2, 7)(
        at, own_valid, log_decay, k, v, gk_local, gv_local, *state_grads
    )
    grad_cross = joined.transpose(1, 2, 0, 3, 4).reshape(2, 2, T, H * DH)
    return grad_q, grad_k, grad_v, grad_cross[0], grad_cross[1]


def solution(mesh):
    rows = P("track", "tm", None)
    return jax.shard_map(
        per_device,
        mesh=mesh,
        in_specs=(rows, rows, rows, P("track", None, "tm"), P(), P("track", None, None, None), rows, rows, rows),
        out_specs=(rows,) * 5,
        check_vma=False,
    )
```

```python
import functools

import jax
import jax.numpy as jnp
from jax import lax
from jax.experimental import pallas as pl
from jax.experimental.pallas import tpu as pltpu
from jax.sharding import PartitionSpec as P

F32, BF16 = jnp.float32, jnp.bfloat16
EPSILON = 1e-06
NEG = -1e30
H, DH = 8, 128
T = 128
NY, NX, NZ = 4, 4, 4
RY = T // NY
PR = DH + 8
PZ = DH + 16
VMEM_LIMIT = 48 * 1024 * 1024

NN = ((1,), (0,))
NT = ((1,), (1,))
TN = ((0,), (0,))


def parts(x):
    if x.dtype == BF16:
        return [x]
    hi = x.astype(BF16)
    return [hi, (x - hi.astype(F32)).astype(BF16)]


def dot(a, b, dims):
    pa, pb = parts(a), parts(b)
    if len(pa) == 2 and len(pb) == 2:
        left, right = [pa[0], pa[0], pa[1]], [pb[0], pb[1], pb[0]]
    else:
        n = max(len(pa), len(pb))
        left = pa * (n // len(pa))
        right = pb * (n // len(pb))
    if len(left) > 1:
        left = jnp.concatenate(left, axis=dims[0][0])
        right = jnp.concatenate(right, axis=dims[1][0])
    else:
        left, right = left[0], right[0]
    return lax.dot_general(left, right, (dims, ((), ())), preferred_element_type=F32)


def sums(ld):
    r = lax.broadcasted_iota(jnp.int32, (T, T), 0)
    c = lax.broadcasted_iota(jnp.int32, (T, T), 1)
    upper = (r <= c).astype(F32)
    lower = (r >= c).astype(F32)
    row = lax.dot_general(
        ld, upper, (NN, ((), ())), precision=lax.Precision.HIGHEST, preferred_element_type=F32
    )
    col = lax.dot_general(
        lower, ld, (NT, ((), ())), precision=lax.Precision.HIGHEST, preferred_element_type=F32
    )
    return row, col, r >= c


def vmem_call(body, out_shape, n_smem, n_in, scratch=(), after=()):
    n = n_smem + n_in

    def ordered(*refs):
        body(*refs[:n], *refs[n + len(after) :])

    call = pl.pallas_call(
        ordered,
        out_shape=out_shape,
        in_specs=[pl.BlockSpec(memory_space=pltpu.SMEM)] * n_smem
        + [pl.BlockSpec(memory_space=pltpu.VMEM)] * n_in
        + [pl.BlockSpec(memory_space=pl.ANY)] * len(after),
        out_specs=jax.tree.map(lambda _: pl.BlockSpec(memory_space=pltpu.VMEM), out_shape),
        scratch_shapes=scratch,
        compiler_params=pltpu.CompilerParams(vmem_limit_bytes=VMEM_LIMIT),
        name=getattr(body, "func", body).__name__,
    )
    return lambda *args: call(*args, *after)


def shape(*dims, dtype=F32):
    return jax.ShapeDtypeStruct(dims, dtype)


def cols(h):
    return slice(h * DH, (h + 1) * DH)


def store_message(ref, h, state, total):
    ref[h, 0:DH, :] = state
    ref[h, DH:PR, :] = jnp.broadcast_to(total, (PR - DH, DH))


def pack_kernel(*refs):
    *ins, out_ref = refs
    for i, one in enumerate(ins):
        for y in range(NY):
            out_ref[y, i] = one[:, y * RY : (y + 1) * RY, :]


def pack(*arrays, after=()):
    n = len(arrays)
    return vmem_call(pack_kernel, shape(NY, n, 2, RY, H * DH, dtype=BF16), 0, n, after=after)(*arrays)


def unpack_kernel(in_ref, *out_refs):
    for i, one in enumerate(out_refs):
        for y in range(NY):
            one[:, y * RY : (y + 1) * RY, :] = in_ref[y, i]


def block_state_kernel(at, valid, ld_ref, k_ref, v_ref, keep_ref, send_ref):
    for i, out_ref in enumerate((keep_ref, send_ref)):
        x = at[0] if i == 0 else 1 - at[0]
        row, col, _ = sums(ld_ref[x])
        for h in range(H):
            scaled = v_ref[x, :, cols(h)].astype(F32) * jnp.exp(col[T - 1 : T, h : h + 1] - col[:, h : h + 1])
            state = dot(k_ref[x, :, cols(h)], scaled, TN)
            store_message(out_ref, h, state * valid[x].astype(F32), row[h : h + 1, T - 1 : T])


def chip_total_kernel(back, at, mine_ref, theirs_ref, *out_refs):
    first = at[0] == (1 if back else 0)
    for q, out_ref in enumerate(out_refs):
        for i in range(2):
            h = 2 * lax.rem(at[1] + q, NX) + i
            mine, theirs = mine_ref[h, DH : DH + 1, :], theirs_ref[h, DH : DH + 1, :]
            a = jnp.where(first, jnp.exp(theirs), 1.0)
            b = jnp.where(first, 1.0, jnp.exp(mine))
            store_message(out_ref, i, a * mine_ref[h, 0:DH, :] + b * theirs_ref[h, 0:DH, :], mine + theirs)


def row_total_kernel(back, at, *refs):
    *in_refs, row_ref, out_ref = refs
    for q, one in enumerate(in_refs):
        row_ref[lax.rem(at[1] - q + NX, NX)] = one[...]
    for p in range(2):
        state, total = None, None
        for j in range(NX - 1, -1, -1) if back else range(NX):
            ld = row_ref[j, p, DH : DH + 1, :]
            if state is None:
                state, total = row_ref[j, p, 0:DH, :], ld
            else:
                state = jnp.exp(ld) * state + row_ref[j, p, 0:DH, :]
                total = total + ld
        high = total.astype(BF16).astype(F32)
        middle = (total - high).astype(BF16).astype(F32)
        r = lax.broadcasted_iota(jnp.int32, (PZ - DH, DH), 0)
        pieces = jnp.where(r == 0, high, jnp.where(r == 1, middle, jnp.where(r == 2, total - high - middle, 0.0)))
        out_ref[p] = jnp.concatenate([state, pieces], axis=0).astype(BF16)


def row_starts_kernel(back, at, *refs):
    if back:
        row_ref, far3, far2, far1, *out_refs, starts = refs
    else:
        init_ref, row_ref, far3, far2, far1, *out_refs, starts = refs
    for p in range(2):
        if back:
            state = jnp.zeros((DH, DH), F32)
        else:
            state = init_ref[at[0], 2 * at[1] + p].astype(F32)
        for far in (far3, far2, far1):
            one = far[p].astype(F32)
            state = jnp.exp(jnp.sum(one[DH:PZ], axis=0, keepdims=True)) * state + one[0:DH]
        for j in range(NX - 1, -1, -1) if back else range(NX):
            starts[j, p] = state
            state = jnp.exp(row_ref[j, p, DH : DH + 1, :]) * state + row_ref[j, p, 0:DH, :]
    for q, out_ref in enumerate(out_refs):
        out_ref[...] = starts[lax.rem(at[1] + q, NX)]


def core_starts_kernel(back, at, *refs):
    *in_refs, mine_ref, theirs_ref, keep_ref, send_ref = refs
    first = at[0] == (1 if back else 0)
    on, off = jnp.where(first, 1.0, 0.0), jnp.where(first, 0.0, 1.0)
    for q, one in enumerate(in_refs):
        for i in range(2):
            h = 2 * lax.rem(at[1] - q + NX, NX) + i
            state = one[i]
            mine, theirs = mine_ref[h, DH : DH + 1, :], theirs_ref[h, DH : DH + 1, :]
            keep_ref[h] = jnp.where(first, 1.0, jnp.exp(theirs)) * state + off * theirs_ref[h, 0:DH, :]
            send_ref[h] = jnp.where(first, jnp.exp(mine), 1.0) * state + on * mine_ref[h, 0:DH, :]


def outputs_kernel(at, valid, ld_ref, q_ref, k_ref, v_ref, *refs):
    *s_refs, out_ref, normed_ref = refs
    for i, s_ref in enumerate(s_refs):
        x = at[0] if i == 0 else 1 - at[0]
        row, col, keep = sums(ld_ref[x])
        flag = valid[x].astype(F32)
        for h in range(H):
            q, k, v = q_ref[x, :, cols(h)], k_ref[x, :, cols(h)], v_ref[x, :, cols(h)]
            decay = jnp.exp(jnp.where(keep, col[:, h : h + 1] - row[h : h + 1, :], -jnp.inf))
            scores = dot(q, k, NT) * (decay * flag)
            out = dot(scores, v, NN) + jnp.exp(col[:, h : h + 1]) * dot(q, s_ref[h], NN)
            inverse = 1.0 / jnp.sqrt(jnp.mean(out * out, axis=-1, keepdims=True) + EPSILON)
            out_ref[x, :, cols(h)] = out
            normed = (out * (inverse * flag)).astype(BF16)
            for y in range(NY):
                normed_ref[y, 0, x, :, cols(h)] = normed[y * RY : (y + 1) * RY, :]


def same_time():
    t = lax.broadcasted_iota(jnp.int32, (16, 256), 0)
    lane = lax.broadcasted_iota(jnp.int32, (16, 256), 1)
    return (lane & 15) == t


def take(ref, g, h, i=0):
    part = ref[:, i, :, g * 16 : (g + 1) * 16, cols(h)]
    return part.reshape(128, DH)


def queries_of(qkg_ref, qx_ref, g, h):
    return jnp.concatenate([take(qkg_ref, g, h, 0), take(qx_ref, g, h)], axis=0)


def grads_of(qkg_ref, gx_ref, g, h):
    return jnp.concatenate([take(qkg_ref, g, h, 2), take(gx_ref, g, h)], axis=0)


def scaled_logits(key_valid, keys, queries):
    logits = (dot(keys, queries, NT) * (1.0 / float(DH) ** 0.5)).reshape(8, 16, 256)
    return [jnp.where(key_valid[j] > 0, logits[j], NEG) for j in range(8)]


def put(ref, g, h, value):
    value = value.astype(ref.dtype).reshape(NY, 2, 16, DH)
    ref[:, 0, :, g * 16 : (g + 1) * 16, cols(h)] = value


def stats_kernel(key_valid, qkg_ref, qx_ref, stats_ref):
    mask = same_time()
    for h in range(H):
        for g in range(RY // 16):
            logits = scaled_logits(key_valid, take(qkg_ref, g, h, 1), queries_of(qkg_ref, qx_ref, g, h))
            top = functools.reduce(jnp.maximum, logits)
            total = functools.reduce(jnp.add, [jnp.exp(one - top) for one in logits])
            r = h * (RY // 16) + g
            stats_ref[0, r : r + 1, :] = jnp.sum(jnp.where(mask, top, 0.0), axis=0, keepdims=True)
            stats_ref[1, r : r + 1, :] = jnp.sum(jnp.where(mask, total, 0.0), axis=0, keepdims=True)


def swap_halves(x):
    return jnp.concatenate([x[:, 128:], x[:, :128]], axis=1)


def weights_of(key_valid, k, q, r, stats_ref, statsx_ref, mask):
    logits = scaled_logits(key_valid, k, q)
    m, mx = stats_ref[0, r : r + 1, :], swap_halves(statsx_ref[0, r : r + 1, :])
    top = jnp.maximum(m, mx)
    total = stats_ref[1, r : r + 1, :] * jnp.exp(m - top)
    total = total + swap_halves(statsx_ref[1, r : r + 1, :]) * jnp.exp(mx - top)
    inverse = 1.0 / total
    return [jnp.where(mask, jnp.exp(one - top) * inverse, 0.0) for one in logits]


def mix_kernel(key_valid, qkg_ref, qx_ref, gx_ref, n_ref, stats_ref, statsx_ref, vi_ref, gn_ref, rd_ref):
    mask = same_time()
    vi = vi_ref[0:1, :]
    for h in range(H):
        for g in range(RY // 16):
            r = h * (RY // 16) + g
            weights = weights_of(
                key_valid, take(qkg_ref, g, h, 1), queries_of(qkg_ref, qx_ref, g, h), r, stats_ref, statsx_ref, mask
            )
            grads = grads_of(qkg_ref, gx_ref, g, h)
            grad_weights = dot(take(n_ref, g, h), grads, NT).reshape(8, 16, 256)
            weights = [one * vi for one in weights]
            put(gn_ref, g, h, dot(jnp.concatenate(weights, axis=0), grads, NN))
            total = functools.reduce(jnp.add, [weights[j] * grad_weights[j] for j in range(8)])
            rd_ref[r : r + 1, :] = jnp.sum(total, axis=0, keepdims=True)


def cross_grads_kernel(
    key_valid, qkg_ref, qx_ref, gx_ref, n_ref, stats_ref, statsx_ref, vi_ref, rd_ref, rdx_ref,
    gk_ref, gq_ref, gqx_ref,
):
    mask = same_time()
    vi = vi_ref[0:1, :]
    for h in range(H):
        for g in range(RY // 16):
            r = h * (RY // 16) + g
            keys, queries = take(qkg_ref, g, h, 1), queries_of(qkg_ref, qx_ref, g, h)
            weights = weights_of(key_valid, keys, queries, r, stats_ref, statsx_ref, mask)
            grads = grads_of(qkg_ref, gx_ref, g, h)
            grad_weights = dot(take(n_ref, g, h), grads, NT).reshape(8, 16, 256)
            along = rd_ref[r : r + 1, :] + swap_halves(rdx_ref[r : r + 1, :])
            scale = vi * (1.0 / float(DH) ** 0.5)
            grad_logits = jnp.concatenate(
                [weights[j] * (grad_weights[j] - along) * scale for j in range(8)], axis=0
            )
            put(gk_ref, g, h, dot(grad_logits, queries, NN))
            grad_queries = dot(grad_logits, keys, TN)
            put(gq_ref, g, h, grad_queries[:128])
            put(gqx_ref, g, h, grad_queries[128:])


def join_kernel(gq_ref, gqx_ref, gk_ref, out_ref):
    for y in range(NY):
        out_ref[y, 0] = (gq_ref[y, 0] + gqx_ref[y, 0].astype(F32)).astype(BF16)
        out_ref[y, 1] = gk_ref[y, 0]


def grad_outputs_kernel(at, valid, ld_ref, q_ref, out_ref, gn_ref, go_ref, keep_ref, send_ref):
    for i, msg_ref in enumerate((keep_ref, send_ref)):
        x = at[0] if i == 0 else 1 - at[0]
        row, col, _ = sums(ld_ref[x])
        flag = valid[x].astype(F32)
        for h in range(H):
            out = out_ref[x, :, cols(h)]
            grad = jnp.concatenate([gn_ref[y, 0, x, :, cols(h)] for y in range(NY)], axis=0).astype(F32)
            inverse = 1.0 / jnp.sqrt(jnp.mean(out * out, axis=-1, keepdims=True) + EPSILON)
            along = jnp.sum(grad * out, axis=-1, keepdims=True)
            go = flag * (inverse * grad - (inverse * inverse * inverse * (1.0 / DH) * along) * out)
            go_ref[x, :, cols(h)] = go
            scaled = go * jnp.exp(col[:, h : h + 1])
            store_message(msg_ref, h, dot(q_ref[x, :, cols(h)], scaled, TN), row[h : h + 1, T - 1 : T])


def local_grads_kernel(at, valid, ld_ref, q_ref, k_ref, v_ref, go_ref, *refs):
    *s_refs, gq_ref, gk_ref, gv_ref = refs
    for i, s_ref in enumerate(s_refs):
        x = at[0] if i == 0 else 1 - at[0]
        row, col, keep = sums(ld_ref[x])
        flag = valid[x].astype(F32)
        for h in range(H):
            q, k, v = q_ref[x, :, cols(h)], k_ref[x, :, cols(h)], v_ref[x, :, cols(h)]
            go = go_ref[x, :, cols(h)]
            decay = jnp.exp(jnp.where(keep, col[:, h : h + 1] - row[h : h + 1, :], -jnp.inf)) * flag
            scores = dot(q, k, NT) * decay
            grad_scores = dot(go, v, NT) * decay
            gq = dot(grad_scores, k, NN) + jnp.exp(col[:, h : h + 1]) * dot(go, s_ref[h], NT)
            gq_ref[x, :, cols(h)] = gq.astype(BF16)
            gk_ref[x, :, cols(h)] = dot(grad_scores, q, TN)
            gv_ref[x, :, cols(h)] = dot(scores, go, TN)


def final_kernel(at, valid, ld_ref, k_ref, v_ref, gk_in, gv_in, *refs):
    *s_refs, gk_ref, gv_ref = refs
    for i, s_ref in enumerate(s_refs):
        x = at[0] if i == 0 else 1 - at[0]
        row, col, _ = sums(ld_ref[x])
        flag = valid[x].astype(F32)
        for h in range(H):
            k, v = k_ref[x, :, cols(h)], v_ref[x, :, cols(h)]
            to_end = jnp.exp(col[T - 1 : T, h : h + 1] - col[:, h : h + 1]) * flag
            state = s_ref[h]
            gk_ref[x, :, cols(h)] = (gk_in[x, :, cols(h)] * flag + to_end * dot(v, state, NT)).astype(BF16)
            gv_ref[x, :, cols(h)] = (gv_in[x, :, cols(h)] * flag + to_end * dot(k, state, NN)).astype(BF16)


YS = [[half * NY + y for y in range(NY)] for half in range(2)]
SWAP = [(i, (i + NY) % (2 * NY)) for i in range(2 * NY)]


def over_y(x):
    return lax.all_to_all(x, "track", 0, 0, axis_index_groups=YS, tiled=True)


def swap(x):
    return lax.ppermute(x, "track", SWAP)


def over_tm(x, to):
    pairs = []
    for i in range(NZ * NX * 2):
        place = to(i // (2 * NX), i // 2 % NX, i % 2)
        if place is not None:
            pairs.append((i, (place[0] * NX + place[1]) * 2 + place[2]))
    return lax.ppermute(x, "tm", pairs)


def core_swap(x):
    return over_tm(x, lambda z, x, c: (z, x, 1 - c))


def x_shift(x, step):
    return over_tm(x, lambda z, x, c: (z, (x + step) % NX, c)) if step else x


def z_shift(x, step):
    return over_tm(x, lambda z, x, c: (z + step, x, c) if 0 <= z + step < NZ else None)


def chip_totals(mine, send, at, back, after=()):
    theirs = core_swap(send)
    totals = vmem_call(functools.partial(chip_total_kernel, back), (shape(2, PR, DH),) * NX, 1, 2, after=after)(
        at, mine, theirs
    )
    return theirs, [x_shift(one, q) for q, one in enumerate(totals)]


def earlier_rows(totals, at, back, after):
    row, total = vmem_call(
        functools.partial(row_total_kernel, back),
        (shape(NX, 2, PR, DH), shape(2, PZ, DH, dtype=BF16)),
        1,
        NX,
        after=after,
    )(at, *totals)
    sign = -1 if back else 1
    return row, [z_shift(total, sign * step) for step in (3, 2, 1)]


def chip_starts(row, far, at, initial, back, after):
    own = () if back else (initial,)
    starts = vmem_call(
        functools.partial(row_starts_kernel, back),
        (shape(2, DH, DH),) * NX,
        1,
        len(own) + 4,
        scratch=[pltpu.VMEM((NX, 2, DH, DH), F32)],
        after=after,
    )(at, *own, row, *far)
    return [x_shift(one, q) for q, one in enumerate(starts)]


def core_starts(starts, mine, theirs, at, back, after=()):
    keep, give = vmem_call(
        functools.partial(core_starts_kernel, back), (shape(H, DH, DH),) * 2, 1, NX + 2, after=after
    )(at, *starts, mine, theirs)
    return keep, core_swap(give)


def per_device(q, k, v, log_decay, valid_length, initial, cross_q, cross_k, grad_out):
    tm, track = lax.axis_index("tm"), lax.axis_index("track")
    half, first = track // NY, tm * T
    alive = (first < valid_length).astype(jnp.int32)
    own_valid = lax.dynamic_slice(alive, (2 * track,), (2,))
    half_valid = lax.dynamic_slice(alive, (8 * half,), (8,))
    other_valid = lax.dynamic_slice(alive, (8 * (1 - half),), (8,))
    lanes = jnp.repeat(jnp.concatenate([half_valid, other_valid]).astype(F32), 16)
    vi = jnp.broadcast_to(lanes[None, :], (8, 256))
    at = jnp.stack([tm % 2, tm // 2 % NX, tm // (2 * NX)]).astype(jnp.int32)

    message = (shape(H, PR, DH),) * 2
    whole = shape(2, T, H * DH)
    half_whole = shape(2, T, H * DH, dtype=BF16)
    quarter = shape(NY, 1, 2, RY, H * DH, dtype=BF16)
    row_stats = shape(RY // 16 * H, 256)
    row_stats2 = shape(2, RY // 16 * H, 256)

    packed = pack(cross_q, cross_k, grad_out)
    qkg = over_y(packed)
    mine, send = vmem_call(block_state_kernel, message, 2, 3, after=(packed,))(at, own_valid, log_decay, k, v)
    theirs, totals = chip_totals(mine, send, at, False)
    row, far = earlier_rows(totals, at, False, ())
    starts = chip_starts(row, far, at, initial, False, (qkg,))
    qkg_, *_ = lax.optimization_barrier((qkg, *far))
    qx, gx = swap(qkg_[:, :1]), swap(qkg_[:, 2:])
    states = core_starts(starts, mine, theirs, at, False)
    out, normed = vmem_call(outputs_kernel, (whole, quarter), 2, 6)(at, own_valid, log_decay, q, k, v, *states)
    stats = vmem_call(stats_kernel, row_stats2, 1, 2)(half_valid, qkg, qx)
    stats_x = swap(stats)
    nx = over_y(normed)
    cross_in = (half_valid, qkg, qx, gx, nx, stats, stats_x, vi)
    gn, rd = vmem_call(mix_kernel, (quarter, row_stats), 1, 7)(*cross_in)
    gn_t = over_y(gn)
    rdx = swap(rd)
    gk_x, gq_own, gq_other = vmem_call(cross_grads_kernel, (quarter, shape(NY, 1, 2, RY, H * DH), quarter), 1, 9)(
        *cross_in, rd, rdx
    )
    gq_back = swap(gq_other)
    go, mine, send = vmem_call(grad_outputs_kernel, (whole, *message), 2, 4, after=(gq_other,))(
        at, own_valid, log_decay, q, out, gn_t
    )
    joined = vmem_call(join_kernel, shape(NY, 2, 2, RY, H * DH, dtype=BF16), 0, 3)(gq_own, gq_back, gk_x)
    joined_y = over_y(joined)
    theirs, totals = chip_totals(mine, send, at, True, (joined,))
    row, far = earlier_rows(totals, at, True, ())
    grad_q, gk_local, gv_local = vmem_call(local_grads_kernel, (half_whole, whole, whole), 2, 7, after=(row,))(
        at, own_valid, log_decay, q, k, v, go, *states
    )
    starts = chip_starts(row, far, at, None, True, (grad_q,))
    grad_cq, grad_ck = vmem_call(unpack_kernel, (half_whole, half_whole), 0, 1)(joined_y)
    state_grads = core_starts(starts, mine, theirs, at, True, (grad_cq,))
    grad_k, grad_v = vmem_call(final_kernel, (half_whole, half_whole), 2, 7)(
        at, own_valid, log_decay, k, v, gk_local, gv_local, *state_grads
    )
    return grad_q, grad_k, grad_v, grad_cq, grad_ck


def solution(mesh):
    rows = P("track", "tm", None)
    return jax.shard_map(
        per_device,
        mesh=mesh,
        in_specs=(rows, rows, rows, P("track", None, "tm"), P(), P("track", None, None, None), rows, rows, rows),
        out_specs=(rows,) * 5,
        check_vma=False,
    )
```

```python
import functools

import jax
import jax.numpy as jnp
from jax import lax
from jax.experimental import pallas as pl
from jax.experimental.pallas import tpu as pltpu
from jax.sharding import PartitionSpec as P

F32, BF16 = jnp.float32, jnp.bfloat16
EPSILON = 1e-06
NEG = -1e30
H, DH = 8, 128
T = 128
NY, NX, NZ = 4, 4, 4
RY = T // NY
PR = DH + 8
PZ = DH + 16
VMEM_LIMIT = 48 * 1024 * 1024

NN = ((1,), (0,))
NT = ((1,), (1,))
TN = ((0,), (0,))


def parts(x):
    if x.dtype == BF16:
        return [x]
    hi = x.astype(BF16)
    return [hi, (x - hi.astype(F32)).astype(BF16)]


def dot(a, b, dims):
    pa, pb = parts(a), parts(b)
    if len(pa) == 2 and len(pb) == 2:
        left, right = [pa[0], pa[0], pa[1]], [pb[0], pb[1], pb[0]]
    else:
        n = max(len(pa), len(pb))
        left = pa * (n // len(pa))
        right = pb * (n // len(pb))
    if len(left) > 1:
        left = jnp.concatenate(left, axis=dims[0][0])
        right = jnp.concatenate(right, axis=dims[1][0])
    else:
        left, right = left[0], right[0]
    return lax.dot_general(left, right, (dims, ((), ())), preferred_element_type=F32)


def sums(ld):
    r = lax.broadcasted_iota(jnp.int32, (T, T), 0)
    c = lax.broadcasted_iota(jnp.int32, (T, T), 1)
    upper = (r <= c).astype(F32)
    lower = (r >= c).astype(F32)
    row = lax.dot_general(
        ld, upper, (NN, ((), ())), precision=lax.Precision.HIGHEST, preferred_element_type=F32
    )
    col = lax.dot_general(
        lower, ld, (NT, ((), ())), precision=lax.Precision.HIGHEST, preferred_element_type=F32
    )
    return row, col, r >= c


def vmem_call(body, out_shape, n_smem, n_in, scratch=(), after=()):
    n = n_smem + n_in

    def ordered(*refs):
        body(*refs[:n], *refs[n + len(after) :])

    call = pl.pallas_call(
        ordered,
        out_shape=out_shape,
        in_specs=[pl.BlockSpec(memory_space=pltpu.SMEM)] * n_smem
        + [pl.BlockSpec(memory_space=pltpu.VMEM)] * n_in
        + [pl.BlockSpec(memory_space=pl.ANY)] * len(after),
        out_specs=jax.tree.map(lambda _: pl.BlockSpec(memory_space=pltpu.VMEM), out_shape),
        scratch_shapes=scratch,
        compiler_params=pltpu.CompilerParams(vmem_limit_bytes=VMEM_LIMIT),
        name=getattr(body, "func", body).__name__,
    )
    return lambda *args: call(*args, *after)


def shape(*dims, dtype=F32):
    return jax.ShapeDtypeStruct(dims, dtype)


def cols(h):
    return slice(h * DH, (h + 1) * DH)


def store_message(ref, h, state, total):
    ref[h, 0:DH, :] = state
    ref[h, DH:PR, :] = jnp.broadcast_to(total, (PR - DH, DH))


def pack_kernel(*refs):
    *ins, out_ref = refs
    for i, one in enumerate(ins):
        for y in range(NY):
            out_ref[y, i] = one[:, y * RY : (y + 1) * RY, :]


def pack(*arrays, after=()):
    n = len(arrays)
    return vmem_call(pack_kernel, shape(NY, n, 2, RY, H * DH, dtype=BF16), 0, n, after=after)(*arrays)


def unpack_kernel(in_ref, *out_refs):
    for i, one in enumerate(out_refs):
        for y in range(NY):
            one[:, y * RY : (y + 1) * RY, :] = in_ref[y, i]


def block_state_kernel(at, valid, ld_ref, k_ref, v_ref, keep_ref, send_ref):
    for i, out_ref in enumerate((keep_ref, send_ref)):
        x = at[0] if i == 0 else 1 - at[0]
        row, col, _ = sums(ld_ref[x])
        for h in range(H):
            scaled = v_ref[x, :, cols(h)].astype(F32) * jnp.exp(col[T - 1 : T, h : h + 1] - col[:, h : h + 1])
            state = dot(k_ref[x, :, cols(h)], scaled, TN)
            store_message(out_ref, h, state * valid[x].astype(F32), row[h : h + 1, T - 1 : T])


def chip_total_kernel(back, at, mine_ref, theirs_ref, *out_refs):
    first = at[0] == (1 if back else 0)
    for q, out_ref in enumerate(out_refs):
        for i in range(2):
            h = 2 * lax.rem(at[1] + q, NX) + i
            mine, theirs = mine_ref[h, DH : DH + 1, :], theirs_ref[h, DH : DH + 1, :]
            a = jnp.where(first, jnp.exp(theirs), 1.0)
            b = jnp.where(first, 1.0, jnp.exp(mine))
            store_message(out_ref, i, a * mine_ref[h, 0:DH, :] + b * theirs_ref[h, 0:DH, :], mine + theirs)


def row_total_kernel(back, at, *refs):
    *in_refs, row_ref, out_ref = refs
    for q, one in enumerate(in_refs):
        row_ref[lax.rem(at[1] - q + NX, NX)] = one[...]
    for p in range(2):
        state, total = None, None
        for j in range(NX - 1, -1, -1) if back else range(NX):
            ld = row_ref[j, p, DH : DH + 1, :]
            if state is None:
                state, total = row_ref[j, p, 0:DH, :], ld
            else:
                state = jnp.exp(ld) * state + row_ref[j, p, 0:DH, :]
                total = total + ld
        high = total.astype(BF16).astype(F32)
        middle = (total - high).astype(BF16).astype(F32)
        r = lax.broadcasted_iota(jnp.int32, (PZ - DH, DH), 0)
        pieces = jnp.where(r == 0, high, jnp.where(r == 1, middle, jnp.where(r == 2, total - high - middle, 0.0)))
        out_ref[p] = jnp.concatenate([state, pieces], axis=0).astype(BF16)


def row_starts_kernel(back, at, *refs):
    if back:
        row_ref, far3, far2, far1, *out_refs, starts = refs
    else:
        init_ref, row_ref, far3, far2, far1, *out_refs, starts = refs
    for p in range(2):
        if back:
            state = jnp.zeros((DH, DH), F32)
        else:
            state = init_ref[at[0], 2 * at[1] + p].astype(F32)
        for far in (far3, far2, far1):
            one = far[p].astype(F32)
            state = jnp.exp(jnp.sum(one[DH:PZ], axis=0, keepdims=True)) * state + one[0:DH]
        for j in range(NX - 1, -1, -1) if back else range(NX):
            starts[j, p] = state
            state = jnp.exp(row_ref[j, p, DH : DH + 1, :]) * state + row_ref[j, p, 0:DH, :]
    for q, out_ref in enumerate(out_refs):
        out_ref[...] = starts[lax.rem(at[1] + q, NX)]


def core_starts_kernel(back, at, *refs):
    *in_refs, mine_ref, theirs_ref, keep_ref, send_ref = refs
    first = at[0] == (1 if back else 0)
    on, off = jnp.where(first, 1.0, 0.0), jnp.where(first, 0.0, 1.0)
    for q, one in enumerate(in_refs):
        for i in range(2):
            h = 2 * lax.rem(at[1] - q + NX, NX) + i
            state = one[i]
            mine, theirs = mine_ref[h, DH : DH + 1, :], theirs_ref[h, DH : DH + 1, :]
            keep_ref[h] = jnp.where(first, 1.0, jnp.exp(theirs)) * state + off * theirs_ref[h, 0:DH, :]
            send_ref[h] = jnp.where(first, jnp.exp(mine), 1.0) * state + on * mine_ref[h, 0:DH, :]


def outputs_kernel(at, valid, ld_ref, q_ref, k_ref, v_ref, *refs):
    *s_refs, out_ref, normed_ref = refs
    for i, s_ref in enumerate(s_refs):
        x = at[0] if i == 0 else 1 - at[0]
        row, col, keep = sums(ld_ref[x])
        flag = valid[x].astype(F32)
        for h in range(H):
            q, k, v = q_ref[x, :, cols(h)], k_ref[x, :, cols(h)], v_ref[x, :, cols(h)]
            decay = jnp.exp(jnp.where(keep, col[:, h : h + 1] - row[h : h + 1, :], -jnp.inf))
            scores = dot(q, k, NT) * (decay * flag)
            out = dot(scores, v, NN) + jnp.exp(col[:, h : h + 1]) * dot(q, s_ref[h], NN)
            inverse = 1.0 / jnp.sqrt(jnp.mean(out * out, axis=-1, keepdims=True) + EPSILON)
            out_ref[x, :, cols(h)] = out
            normed = (out * (inverse * flag)).astype(BF16)
            for y in range(NY):
                normed_ref[y, 0, x, :, cols(h)] = normed[y * RY : (y + 1) * RY, :]


def same_time():
    t = lax.broadcasted_iota(jnp.int32, (16, 256), 0)
    lane = lax.broadcasted_iota(jnp.int32, (16, 256), 1)
    return (lane & 15) == t


def take(ref, g, h, i=0):
    part = ref[:, i, :, g * 16 : (g + 1) * 16, cols(h)]
    return part.reshape(128, DH)


def queries_of(qkg_ref, qx_ref, g, h):
    return jnp.concatenate([take(qkg_ref, g, h, 0), take(qx_ref, g, h)], axis=0)


def grads_of(qkg_ref, gx_ref, g, h):
    return jnp.concatenate([take(qkg_ref, g, h, 2), take(gx_ref, g, h)], axis=0)


def scaled_logits(key_valid, keys, queries):
    logits = (dot(keys, queries, NT) * (1.0 / float(DH) ** 0.5)).reshape(8, 16, 256)
    return [jnp.where(key_valid[j] > 0, logits[j], NEG) for j in range(8)]


def put(ref, g, h, value):
    value = value.astype(ref.dtype).reshape(NY, 2, 16, DH)
    ref[:, 0, :, g * 16 : (g + 1) * 16, cols(h)] = value


def stats_kernel(key_valid, qkg_ref, qx_ref, stats_ref):
    mask = same_time()
    for h in range(H):
        for g in range(RY // 16):
            logits = scaled_logits(key_valid, take(qkg_ref, g, h, 1), queries_of(qkg_ref, qx_ref, g, h))
            top = functools.reduce(jnp.maximum, logits)
            total = functools.reduce(jnp.add, [jnp.exp(one - top) for one in logits])
            r = h * (RY // 16) + g
            stats_ref[0, r : r + 1, :] = jnp.sum(jnp.where(mask, top, 0.0), axis=0, keepdims=True)
            stats_ref[1, r : r + 1, :] = jnp.sum(jnp.where(mask, total, 0.0), axis=0, keepdims=True)


def swap_halves(x):
    return jnp.concatenate([x[:, 128:], x[:, :128]], axis=1)


def weights_of(key_valid, k, q, r, stats_ref, statsx_ref, mask):
    logits = scaled_logits(key_valid, k, q)
    m, mx = stats_ref[0, r : r + 1, :], swap_halves(statsx_ref[0, r : r + 1, :])
    top = jnp.maximum(m, mx)
    total = stats_ref[1, r : r + 1, :] * jnp.exp(m - top)
    total = total + swap_halves(statsx_ref[1, r : r + 1, :]) * jnp.exp(mx - top)
    inverse = 1.0 / total
    return [jnp.where(mask, jnp.exp(one - top) * inverse, 0.0) for one in logits]


def mix_kernel(key_valid, qkg_ref, qx_ref, gx_ref, n_ref, stats_ref, statsx_ref, vi_ref, gn_ref, rd_ref):
    mask = same_time()
    vi = vi_ref[0:1, :]
    for h in range(H):
        for g in range(RY // 16):
            r = h * (RY // 16) + g
            weights = weights_of(
                key_valid, take(qkg_ref, g, h, 1), queries_of(qkg_ref, qx_ref, g, h), r, stats_ref, statsx_ref, mask
            )
            grads = grads_of(qkg_ref, gx_ref, g, h)
            grad_weights = dot(take(n_ref, g, h), grads, NT).reshape(8, 16, 256)
            weights = [one * vi for one in weights]
            put(gn_ref, g, h, dot(jnp.concatenate(weights, axis=0), grads, NN))
            total = functools.reduce(jnp.add, [weights[j] * grad_weights[j] for j in range(8)])
            rd_ref[r : r + 1, :] = jnp.sum(total, axis=0, keepdims=True)


def cross_grads_kernel(
    key_valid, qkg_ref, qx_ref, gx_ref, n_ref, stats_ref, statsx_ref, vi_ref, rd_ref, rdx_ref,
    gk_ref, gq_ref, gqx_ref,
):
    mask = same_time()
    vi = vi_ref[0:1, :]
    for h in range(H):
        for g in range(RY // 16):
            r = h * (RY // 16) + g
            keys, queries = take(qkg_ref, g, h, 1), queries_of(qkg_ref, qx_ref, g, h)
            weights = weights_of(key_valid, keys, queries, r, stats_ref, statsx_ref, mask)
            grads = grads_of(qkg_ref, gx_ref, g, h)
            grad_weights = dot(take(n_ref, g, h), grads, NT).reshape(8, 16, 256)
            along = rd_ref[r : r + 1, :] + swap_halves(rdx_ref[r : r + 1, :])
            scale = vi * (1.0 / float(DH) ** 0.5)
            grad_logits = jnp.concatenate(
                [weights[j] * (grad_weights[j] - along) * scale for j in range(8)], axis=0
            )
            put(gk_ref, g, h, dot(grad_logits, queries, NN))
            grad_queries = dot(grad_logits, keys, TN)
            put(gq_ref, g, h, grad_queries[:128])
            put(gqx_ref, g, h, grad_queries[128:])


def join_kernel(gq_ref, gqx_ref, gk_ref, out_ref):
    for y in range(NY):
        out_ref[y, 0] = (gq_ref[y, 0] + gqx_ref[y, 0].astype(F32)).astype(BF16)
        out_ref[y, 1] = gk_ref[y, 0]


def grad_outputs_kernel(at, valid, ld_ref, q_ref, out_ref, gn_ref, go_ref, keep_ref, send_ref):
    for i, msg_ref in enumerate((keep_ref, send_ref)):
        x = at[0] if i == 0 else 1 - at[0]
        row, col, _ = sums(ld_ref[x])
        flag = valid[x].astype(F32)
        for h in range(H):
            out = out_ref[x, :, cols(h)]
            grad = jnp.concatenate([gn_ref[y, 0, x, :, cols(h)] for y in range(NY)], axis=0).astype(F32)
            inverse = 1.0 / jnp.sqrt(jnp.mean(out * out, axis=-1, keepdims=True) + EPSILON)
            along = jnp.sum(grad * out, axis=-1, keepdims=True)
            go = flag * (inverse * grad - (inverse * inverse * inverse * (1.0 / DH) * along) * out)
            go_ref[x, :, cols(h)] = go
            scaled = go * jnp.exp(col[:, h : h + 1])
            store_message(msg_ref, h, dot(q_ref[x, :, cols(h)], scaled, TN), row[h : h + 1, T - 1 : T])


def local_grads_kernel(at, valid, ld_ref, q_ref, k_ref, v_ref, go_ref, *refs):
    *s_refs, gq_ref, gk_ref, gv_ref = refs
    for i, s_ref in enumerate(s_refs):
        x = at[0] if i == 0 else 1 - at[0]
        row, col, keep = sums(ld_ref[x])
        flag = valid[x].astype(F32)
        for h in range(H):
            q, k, v = q_ref[x, :, cols(h)], k_ref[x, :, cols(h)], v_ref[x, :, cols(h)]
            go = go_ref[x, :, cols(h)]
            decay = jnp.exp(jnp.where(keep, col[:, h : h + 1] - row[h : h + 1, :], -jnp.inf)) * flag
            scores = dot(q, k, NT) * decay
            grad_scores = dot(go, v, NT) * decay
            gq = dot(grad_scores, k, NN) + jnp.exp(col[:, h : h + 1]) * dot(go, s_ref[h], NT)
            gq_ref[x, :, cols(h)] = gq.astype(BF16)
            gk_ref[x, :, cols(h)] = dot(grad_scores, q, TN)
            gv_ref[x, :, cols(h)] = dot(scores, go, TN)


def final_kernel(at, valid, ld_ref, k_ref, v_ref, gk_in, gv_in, *refs):
    *s_refs, gk_ref, gv_ref = refs
    for i, s_ref in enumerate(s_refs):
        x = at[0] if i == 0 else 1 - at[0]
        row, col, _ = sums(ld_ref[x])
        flag = valid[x].astype(F32)
        for h in range(H):
            k, v = k_ref[x, :, cols(h)], v_ref[x, :, cols(h)]
            to_end = jnp.exp(col[T - 1 : T, h : h + 1] - col[:, h : h + 1]) * flag
            state = s_ref[h]
            gk_ref[x, :, cols(h)] = (gk_in[x, :, cols(h)] * flag + to_end * dot(v, state, NT)).astype(BF16)
            gv_ref[x, :, cols(h)] = (gv_in[x, :, cols(h)] * flag + to_end * dot(k, state, NN)).astype(BF16)


YS = [[half * NY + y for y in range(NY)] for half in range(2)]
SWAP = [(i, (i + NY) % (2 * NY)) for i in range(2 * NY)]


def over_y(x):
    return lax.all_to_all(x, "track", 0, 0, axis_index_groups=YS, tiled=True)


def swap(x):
    return lax.ppermute(x, "track", SWAP)


def over_tm(x, to):
    pairs = []
    for i in range(NZ * NX * 2):
        place = to(i // (2 * NX), i // 2 % NX, i % 2)
        if place is not None:
            pairs.append((i, (place[0] * NX + place[1]) * 2 + place[2]))
    return lax.ppermute(x, "tm", pairs)


def core_swap(x):
    return over_tm(x, lambda z, x, c: (z, x, 1 - c))


def x_shift(x, step):
    return over_tm(x, lambda z, x, c: (z, (x + step) % NX, c)) if step else x


def z_shift(x, step):
    return over_tm(x, lambda z, x, c: (z + step, x, c) if 0 <= z + step < NZ else None)


def chip_totals(mine, send, at, back, after=()):
    theirs = core_swap(send)
    totals = vmem_call(functools.partial(chip_total_kernel, back), (shape(2, PR, DH),) * NX, 1, 2, after=after)(
        at, mine, theirs
    )
    return theirs, [x_shift(one, q) for q, one in enumerate(totals)]


def earlier_rows(totals, at, back, after):
    row, total = vmem_call(
        functools.partial(row_total_kernel, back),
        (shape(NX, 2, PR, DH), shape(2, PZ, DH, dtype=BF16)),
        1,
        NX,
        after=after,
    )(at, *totals)
    sign = -1 if back else 1
    return row, [z_shift(total, sign * step) for step in (3, 2, 1)]


def chip_starts(row, far, at, initial, back, after):
    own = () if back else (initial,)
    starts = vmem_call(
        functools.partial(row_starts_kernel, back),
        (shape(2, DH, DH),) * NX,
        1,
        len(own) + 4,
        scratch=[pltpu.VMEM((NX, 2, DH, DH), F32)],
        after=after,
    )(at, *own, row, *far)
    return [x_shift(one, q) for q, one in enumerate(starts)]


def core_starts(starts, mine, theirs, at, back, after=()):
    keep, give = vmem_call(
        functools.partial(core_starts_kernel, back), (shape(H, DH, DH),) * 2, 1, NX + 2, after=after
    )(at, *starts, mine, theirs)
    return keep, core_swap(give)


def per_device(q, k, v, log_decay, valid_length, initial, cross_q, cross_k, grad_out):
    tm, track = lax.axis_index("tm"), lax.axis_index("track")
    half, first = track // NY, tm * T
    alive = (first < valid_length).astype(jnp.int32)
    own_valid = lax.dynamic_slice(alive, (2 * track,), (2,))
    half_valid = lax.dynamic_slice(alive, (8 * half,), (8,))
    other_valid = lax.dynamic_slice(alive, (8 * (1 - half),), (8,))
    lanes = jnp.repeat(jnp.concatenate([half_valid, other_valid]).astype(F32), 16)
    vi = jnp.broadcast_to(lanes[None, :], (8, 256))
    at = jnp.stack([tm % 2, tm // 2 % NX, tm // (2 * NX)]).astype(jnp.int32)

    message = (shape(H, PR, DH),) * 2
    whole = shape(2, T, H * DH)
    half_whole = shape(2, T, H * DH, dtype=BF16)
    quarter = shape(NY, 1, 2, RY, H * DH, dtype=BF16)
    row_stats = shape(RY // 16 * H, 256)
    row_stats2 = shape(2, RY // 16 * H, 256)

    packed = pack(cross_q, cross_k, grad_out)
    qkg = over_y(packed)
    mine, send = vmem_call(block_state_kernel, message, 2, 3, after=(packed,))(at, own_valid, log_decay, k, v)
    theirs, totals = chip_totals(mine, send, at, False)
    row, far = earlier_rows(totals, at, False, ())
    starts = chip_starts(row, far, at, initial, False, (qkg,))
    qkg_, *_ = lax.optimization_barrier((qkg, *far))
    qx, gx = swap(qkg_[:, :1]), swap(qkg_[:, 2:])
    states = core_starts(starts, mine, theirs, at, False, (qx,))
    out, normed = vmem_call(outputs_kernel, (whole, quarter), 2, 6)(at, own_valid, log_decay, q, k, v, *states)
    stats = vmem_call(stats_kernel, row_stats2, 1, 2)(half_valid, qkg, qx)
    stats_x = swap(stats)
    nx = over_y(normed)
    cross_in = (half_valid, qkg, qx, gx, nx, stats, stats_x, vi)
    gn, rd = vmem_call(mix_kernel, (quarter, row_stats), 1, 7)(*cross_in)
    gn_t = over_y(gn)
    rdx = swap(rd)
    gk_x, gq_own, gq_other = vmem_call(cross_grads_kernel, (quarter, shape(NY, 1, 2, RY, H * DH), quarter), 1, 9)(
        *cross_in, rd, rdx
    )
    gq_back = swap(gq_other)
    go, mine, send = vmem_call(grad_outputs_kernel, (whole, *message), 2, 4, after=(gq_other,))(
        at, own_valid, log_decay, q, out, gn_t
    )
    joined = vmem_call(join_kernel, shape(NY, 2, 2, RY, H * DH, dtype=BF16), 0, 3)(gq_own, gq_back, gk_x)
    joined_y = over_y(joined)
    theirs, totals = chip_totals(mine, send, at, True, (joined,))
    row, far = earlier_rows(totals, at, True, ())
    grad_q, gk_local, gv_local = vmem_call(local_grads_kernel, (half_whole, whole, whole), 2, 7, after=(row,))(
        at, own_valid, log_decay, q, k, v, go, *states
    )
    starts = chip_starts(row, far, at, None, True, (grad_q,))
    grad_cq, grad_ck = vmem_call(unpack_kernel, (half_whole, half_whole), 0, 1)(joined_y)
    state_grads = core_starts(starts, mine, theirs, at, True, (grad_cq,))
    grad_k, grad_v = vmem_call(final_kernel, (half_whole, half_whole), 2, 7)(
        at, own_valid, log_decay, k, v, gk_local, gv_local, *state_grads
    )
    return grad_q, grad_k, grad_v, grad_cq, grad_ck


def solution(mesh):
    rows = P("track", "tm", None)
    return jax.shard_map(
        per_device,
        mesh=mesh,
        in_specs=(rows, rows, rows, P("track", None, "tm"), P(), P("track", None, None, None), rows, rows, rows),
        out_specs=(rows,) * 5,
        check_vma=False,
    )
```
